256 devices in a mesh: wide: 32 (over x, z), narrow: 8 (over y, core).
Axes of the slice: x: 4, y: 4, z: 8, core: 2. Of those that a mesh axis runs over, the one named last changes fastest.
Arguments:
- hidden: bfloat16 [2, 2048, 8192], P(None, 'wide', 'narrow'), may hold values from -6 to 6
- router_weight: float32 [8192], P('narrow'), may hold values from -0.0625 to 0.0625
- teacher: float32 [2, 2048], P(None, 'wide'), may hold values from 0.05 to 0.95
- positions: int32 [2, 256], replicated, may hold values from 0 to 2047, as said below
- cotangent: bfloat16 [2, 256, 8192], P(None, 'wide', 'narrow'), may hold values from -6 to 6
- gate_weight: bfloat16 [8192, 28672], P('narrow', 'wide'), may hold values from -0.0625 to 0.0625
- up_weight: bfloat16 [8192, 28672], P('narrow', 'wide'), may hold values from -0.0625 to 0.0625
- down_weight: bfloat16 [28672, 8192], P('wide', 'narrow'), may hold values from -0.03125 to 0.03125
Outputs:
- hidden_grad: bfloat16 [2, 2048, 8192], P(None, 'wide', 'narrow')
- router_grad: float32 [8192], P('narrow')
- gate_grad: bfloat16 [8192, 28672], P('narrow', 'wide')
- up_grad: bfloat16 [8192, 28672], P('narrow', 'wide')
- down_grad: bfloat16 [28672, 8192], P('wide', 'narrow')
The draws below stay inside these ranges and needn't reach their ends.
Inputs may be any that keep to these rules, and one draw needn't show every extreme that they name: In each slab the positions rise strictly, and every aligned block of 64 slab positions holds exactly 8 of them.
All inputs are finite; a program needn't handle non-finite values.
Results may differ from the reference program's by a relative error of at most 0.0058.
Values may be sent and summed in bfloat16 or wider, within the bound.
A program may use at most 64 MiB of HBM per device.

```python
import jax
import jax.numpy as jnp
from jax import lax

D = 8192
FF = 28672
ROWS_DEV = 64
SLABS = 2
ROUTED_DEV = 8
SLAB = 2048
ROUTED = 256
N_WIDE = 32


def draw_positions(key, part):
    key = jax.random.fold_in(key, 11)
    scores = jax.random.randint(key, (SLABS, N_WIDE, ROWS_DEV), 0, 1 << 20)
    scores = scores * ROWS_DEV + jnp.arange(ROWS_DEV, dtype=jnp.int32)[None, None, :]
    block_ids = jnp.arange(N_WIDE, dtype=jnp.int32)[:, None]
    row_ids = jnp.arange(ROWS_DEV, dtype=jnp.int32)[None, :]
    forced = (block_ids == 0) & (row_ids == 0) | (block_ids == N_WIDE - 1) & (row_ids == ROWS_DEV - 1)
    scores = scores - (forced.astype(jnp.int32) * (1 << 29))[None, :, :]
    picked = jnp.argsort(scores, axis=-1)[:, :, :ROUTED_DEV]
    picked = jnp.sort(picked, axis=-1).astype(jnp.int32)
    offsets = (jnp.arange(N_WIDE, dtype=jnp.int32) * ROWS_DEV)[None, :, None]
    return (picked + offsets).reshape(SLABS, ROUTED_DEV * N_WIDE).astype(jnp.int32)


def levels(rng, extent, cuts, least, largest):
    def one(position, parts):
        draws = jax.random.uniform(jax.random.fold_in(jax.random.fold_in(rng, 6), position), (parts,), jnp.float32, least / len(cuts), largest / len(cuts))
        return jnp.repeat(jnp.exp(draws), extent[position] // parts).reshape((-1,) + (1,) * (len(extent) - position - 1))

    level = one(*cuts[0])
    for cut in cuts[1:]:
        level = level * one(*cut)
    return level


def gaussian(rng, dims, deviation, reach, shards=(), held_as=jnp.bfloat16):
    entries = deviation * jax.random.normal(rng, dims, jnp.float32)
    if shards:
        entries = entries * levels(rng, dims, shards, -0.22, 0.18)
    return jnp.clip(entries, -reach, reach).astype(held_as)


def setup_inputs(seed: int = 0) -> dict:
    key_list = jax.random.split(jax.random.key(seed), 9)
    return {
        "hidden": gaussian(key_list[0], (SLABS, SLAB, D), 1.0, 6.0, ((1, 32), (2, 8))),
        "router_weight": gaussian(key_list[1], (D,), D ** -0.5, 0.0625, ((0, 8),), jnp.float32),
        "teacher": jnp.clip(0.05 + 0.9 * jax.random.uniform(key_list[2], (SLABS, SLAB), jnp.float32) ** levels(key_list[2], (SLABS, SLAB), ((1, 32),), -0.2, 0.2), 0.05, 0.95),
        "positions": draw_positions(jax.random.fold_in(key_list[8], 71), 0),
        "cotangent": gaussian(key_list[4], (SLABS, ROUTED, D), 1.0, 6.0, ((1, 32), (2, 8))),
        "gate_weight": gaussian(key_list[5], (D, FF), D ** -0.5, 0.0625, ((0, 8), (1, 32))),
        "up_weight": gaussian(key_list[6], (D, FF), D ** -0.5, 0.0625, ((0, 8), (1, 32))),
        "down_weight": gaussian(key_list[7], (FF, D), FF ** -0.5, 0.03125, ((0, 32), (1, 8))),
    }


def reference(hidden, router_weight, teacher, positions, cotangent, gate_weight, up_weight, down_weight):
    slabs = hidden.shape[0]
    hidden32 = hidden.astype(jnp.float32)
    logits = jnp.einsum("snd,d->sn", hidden32, router_weight, precision=lax.Precision.HIGHEST)
    slab_index = jnp.arange(slabs, dtype=jnp.int32)[:, None]
    rows = hidden[slab_index, positions].reshape(-1, D)
    gate = jnp.dot(rows, gate_weight, preferred_element_type=jnp.float32)
    up = jnp.dot(rows, up_weight, preferred_element_type=jnp.float32)
    sig = jax.nn.sigmoid(gate)
    act = (gate * sig * up).astype(jnp.bfloat16)
    mlp_out = jnp.dot(act, down_weight, preferred_element_type=jnp.float32)
    scale = jax.nn.sigmoid(logits[slab_index, positions])
    cot32 = cotangent.astype(jnp.float32)
    dots = jnp.sum(cot32 * mlp_out.reshape(cot32.shape), axis=-1)
    out_grad = (scale[:, :, None] * cot32).astype(jnp.bfloat16).reshape(-1, D)
    down_grad = lax.dot_general(act, out_grad, (((0,), (0,)), ((), ())), preferred_element_type=jnp.float32).astype(jnp.bfloat16)
    act_grad = lax.dot_general(out_grad, down_weight, (((1,), (1,)), ((), ())), preferred_element_type=jnp.float32)
    gate_pre = (act_grad * up * sig * (1.0 + gate * (1.0 - sig))).astype(jnp.bfloat16)
    up_pre = (act_grad * gate * sig).astype(jnp.bfloat16)
    gate_grad = lax.dot_general(rows, gate_pre, (((0,), (0,)), ((), ())), preferred_element_type=jnp.float32).astype(jnp.bfloat16)
    up_grad = lax.dot_general(rows, up_pre, (((0,), (0,)), ((), ())), preferred_element_type=jnp.float32).astype(jnp.bfloat16)
    rows_grad = lax.dot_general(gate_pre, gate_weight, (((1,), (1,)), ((), ())), preferred_element_type=jnp.float32)
    rows_grad = rows_grad + lax.dot_general(up_pre, up_weight, (((1,), (1,)), ((), ())), preferred_element_type=jnp.float32)
    logit_grad = jax.nn.sigmoid(logits) - teacher
    logit_grad = logit_grad.at[slab_index, positions].add(scale * (1.0 - scale) * dots)
    hidden_grad = logit_grad[:, :, None] * router_weight[None, None, :]
    hidden_grad = hidden_grad.at[slab_index, positions].add(rows_grad.reshape(cot32.shape))
    router_grad = jnp.einsum("sn,snd->d", logit_grad, hidden32, precision=lax.Precision.HIGHEST)
    return hidden_grad.astype(jnp.bfloat16), router_grad, gate_grad, up_grad, down_grad
```

```python
import functools

import jax
import jax.numpy as jnp
from jax import lax
from jax.experimental import pallas as pl
from jax.experimental.pallas import tpu as pltpu
from jax.sharding import PartitionSpec as P

MESH = pl.DeviceIdType.MESH
F32 = jnp.float32
BF16 = jnp.bfloat16

NX, NZ, NY = 4, 8, 4
TOK = 128
OWN = 16
ROWS = OWN * NX * NZ
SLOT = OWN * NX
CH = 2 * SLOT
NCH = ROWS // CH
EXT = 128
OFFSETS = (0, 1, -1, 2, -2, 3, -3, 4)


def encode(value, rows):
    wide = jnp.broadcast_to(value, (rows, EXT))
    high = wide.astype(BF16).astype(F32)
    lane = lax.broadcasted_iota(jnp.int32, (rows, EXT), 1)
    return jnp.where(lane < EXT // 2, high, wide - high).astype(BF16)


def decode(block):
    return block[:, 0:1].astype(F32) + block[:, EXT // 2 : EXT // 2 + 1].astype(F32)


def nt(a, b):
    return lax.dot_general(a, b, (((1,), (1,)), ((), ())), preferred_element_type=F32)


def tn(a, b):
    return lax.dot_general(a, b, (((0,), (0,)), ((), ())), preferred_element_type=F32)


def tiles(extent, step):
    return [(at, min(step, extent - at)) for at in range(0, extent, step)]


def kernel(
    D,
    F,
    hidden_hbm,
    rw_ref,
    teacher_ref,
    pos_ref,
    cot_ref,
    gw_hbm,
    uw_hbm,
    dw_hbm,
    hg_hbm,
    rg_ref,
    gg_hbm,
    ug_hbm,
    dg_hbm,
    hid,
    wgu,
    wd,
    agb,
    part,
    csend,
    crecv,
    ysend,
    yfirst,
    ysecond,
    ysum,
    gact,
    rgf,
    xsend,
    xrecv,
    zown,
    zsend,
    zrecv,
    lsend,
    lrecv,
    rparts_x,
    rparts_z,
    hg_out,
    gg_out,
    ug_out,
    dg_out,
    send_sem,
    recv_sem,
    local_sem,
):
    C = 3 * F + EXT
    H = C // 2
    wide, narrow = lax.axis_index("wide"), lax.axis_index("narrow")
    x, z = lax.div(wide, NZ), lax.rem(wide, NZ)
    y, core = lax.div(narrow, 2), lax.rem(narrow, 2)

    def at_x(d):
        return (lax.rem(x + d + NX, NX) * NZ + z, narrow)

    def at_z(d):
        return (x * NZ + lax.rem(z + d + NZ, NZ), narrow)

    def at_y(d):
        return (wide, lax.rem(y + d + NY, NY) * 2 + core)

    def at_n(d):
        return (wide, lax.rem(narrow + d, 2 * NY))

    sibling = (wide, y * 2 + (1 - core))

    count = [0]
    started = []

    def send(src, dst, device):
        i = count[0]
        count[0] += 1
        copy = pltpu.make_async_remote_copy(
            src_ref=src,
            dst_ref=dst,
            send_sem=send_sem.at[i],
            recv_sem=recv_sem.at[i],
            device_id=device,
            device_id_type=MESH,
        )
        copy.start()
        started.append(copy)
        return copy

    lcount = [0]

    def local(src, dst):
        copy = pltpu.make_async_copy(src, dst, local_sem.at[lcount[0]])
        lcount[0] += 1
        copy.start()
        return copy

    load_hid = local(hidden_hbm, hid)
    load_w = [
        local(gw_hbm, wgu.at[:, pl.ds(0, F)]),
        local(uw_hbm, wgu.at[:, pl.ds(F, F)]),
        local(dw_hbm, wd),
    ]

    barrier = pltpu.get_barrier_semaphore()
    peers = (
        [at_x(d) for d in range(1, NX)]
        + [at_z(d) for d in range(1, NZ)]
        + [at_n(d) for d in range(1, 2 * NY)]
    )
    for peer in peers:
        pl.semaphore_signal(barrier, inc=1, device_id=peer, device_id_type=MESH)

    sub = lax.broadcasted_iota(jnp.int32, (OWN, TOK), 0)
    lane = lax.broadcasted_iota(jnp.int32, (OWN, TOK), 1)
    sub_t = lax.broadcasted_iota(jnp.int32, (TOK, OWN), 0)
    lane_t = lax.broadcasted_iota(jnp.int32, (TOK, OWN), 1)
    pick = jnp.zeros((OWN, TOK), F32)
    place = jnp.zeros((TOK, OWN), F32)
    half_own, half_tok = OWN // 2, TOK // 2
    for r in range(OWN):
        s, j = r // half_own, r % half_own
        token = pos_ref[s, wide * half_own + j] - wide * half_tok + s * half_tok
        pick = jnp.where((sub == r) & (lane == token), 1.0, pick)
        place = jnp.where((lane_t == r) & (sub_t == token), 1.0, place)
    load_hid.wait()
    own_rows = jnp.dot(pick.astype(BF16), hid[...], preferred_element_type=F32)
    agb[0, pl.ds(0, OWN), :] = own_rows.astype(BF16)
    agb[1, pl.ds(0, OWN), :] = jnp.concatenate(
        [cot_ref[0].astype(F32), cot_ref[1].astype(F32)], axis=0
    ).astype(BF16)
    pl.semaphore_wait(barrier, len(peers))

    gx = [
        send(
            agb.at[:, pl.ds(0, OWN)],
            agb.at[:, pl.ds((NX - d) * OWN, OWN)],
            at_x(d),
        )
        for d in (1, 3, 2)
    ]

    eye = lax.broadcasted_iota(jnp.int32, (TOK, TOK), 0) == lax.broadcasted_iota(
        jnp.int32, (TOK, TOK), 1
    )
    logit_col = jnp.sum(hid[...].astype(F32) * rw_ref[...], axis=1, keepdims=True)
    logit_row = jnp.sum(jnp.where(eye, logit_col, 0.0), axis=0, keepdims=True)
    lsend[...] = jnp.broadcast_to(logit_row, (8, TOK))
    lg = [send(lsend, lrecv.at[d - 1], at_n(d)) for d in range(1, 2 * NY)]

    for copy in gx:
        copy.wait_recv()

    def slot(k, n=1):
        return pl.ds(k * SLOT, n * SLOT)

    def gather_z(src, dst, d, which=None):
        if which is None:
            return send(agb.at[:, slot(src)], agb.at[:, slot(dst)], at_z(d))
        return send(agb.at[which, slot(src)], agb.at[which, slot(dst)], at_z(d))

    gz = {0: [gather_z(0, 1, -1), gather_z(0, 2, 1)]}
    for copy in load_w:
        copy.wait()

    core_out, y_first, y_second, g_first, g_second, core_back, x_out, z_out = (
        {} for _ in range(8)
    )

    def block(j, base=0):
        return pl.ds(pl.multiple_of(base + lax.rem(y + j + NY, NY) * OWN, OWN), OWN)

    def stage1(i):
        for copy in gz[i]:
            copy.wait_recv()
        if i == 0:
            gz[1] = [gather_z(1, 3, -1), gather_z(2, 4, 1)]
        elif i == 1:
            gz[2] = [gather_z(3, 5, -1), gather_z(4, 6, 1)]
        elif i == 2:
            gz[3] = [gather_z(5, 7, -1, 0), gather_z(6, 7, 1, 1)]
        rows = pl.ds(i * CH, CH)

        @pl.loop(0, 2 * F // 256)
        def _(t):
            cols = pl.ds(pl.multiple_of(t * 256, 256), 256)
            part[i, :, cols] = jnp.dot(
                agb[0, rows, :], wgu[:, cols], preferred_element_type=F32
            )

        for at, n in tiles(F, 256):
            part[i, :, pl.ds(2 * F + at, n)] = nt(agb[1, rows, :], wd[pl.ds(at, n), :])
        logit = jnp.sum(agb[0, rows, :].astype(F32) * rw_ref[...], axis=1, keepdims=True)
        part[i, :, pl.ds(3 * F, EXT)] = jnp.broadcast_to(logit, (CH, EXT))
        other = pl.ds(pl.multiple_of((1 - core) * SLOT, SLOT), SLOT)
        csend[i, :, pl.ds(0, 3 * F)] = part[i, other, pl.ds(0, 3 * F)].astype(BF16)
        csend[i, :, pl.ds(3 * F, EXT)] = encode(
            part[i, other, pl.ds(3 * F, EXT)][:, 0:1], SLOT
        )
        core_out[i] = send(csend.at[i], crecv.at[i], sibling)

    def stage2(i):
        core_out[i].wait_recv()
        base = pl.multiple_of(core * SLOT, SLOT)
        mine = pl.ds(base, SLOT)
        total = part[i, mine, pl.ds(0, 3 * F)] + crecv[i, :, pl.ds(0, 3 * F)].astype(F32)
        part[i, mine, pl.ds(0, 3 * F)] = total
        ysend[i, :, pl.ds(0, 3 * F)] = total.astype(BF16)
        logit = part[i, mine, pl.ds(3 * F, EXT)][:, 0:1] + decode(
            crecv[i, :, pl.ds(3 * F, EXT)]
        )
        part[i, mine, pl.ds(3 * F, EXT)] = jnp.broadcast_to(logit, (SLOT, EXT))
        ysend[i, :, pl.ds(3 * F, EXT)] = encode(logit, SLOT)
        left, right = pl.ds(0, H), pl.ds(H, H)
        y_first[i] = [
            send(ysend.at[i, block(2), left], yfirst.at[i, 0], at_y(1)),
            send(ysend.at[i, block(2), right], yfirst.at[i, 1], at_y(-1)),
            send(ysend.at[i, block(1), right], ysecond.at[i, 0, :, right], at_y(1)),
            send(ysend.at[i, block(-1), left], ysecond.at[i, 1, :, left], at_y(-1)),
        ]

    def stage3(i):
        y_first[i][0].wait_recv()
        y_first[i][1].wait_recv()
        base = core * SLOT
        left, right = pl.ds(0, H), pl.ds(H, H)
        ysum[i, 0] = (
            part[i, block(1, base), left] + yfirst[i, 0].astype(F32)
        ).astype(BF16)
        a = send(ysum.at[i, 0], ysecond.at[i, 0, :, left], at_y(1))
        ysum[i, 1, :, pl.ds(0, H - EXT)] = (
            part[i, block(-1, base), pl.ds(H, H - EXT)]
            + yfirst[i, 1, :, pl.ds(0, H - EXT)].astype(F32)
        ).astype(BF16)
        logit = part[i, block(-1, base), pl.ds(3 * F, EXT)][:, 0:1] + decode(
            yfirst[i, 1, :, pl.ds(H - EXT, EXT)]
        )
        ysum[i, 1, :, pl.ds(H - EXT, EXT)] = encode(logit, OWN)
        b = send(ysum.at[i, 1], ysecond.at[i, 1, :, right], at_y(-1))
        y_second[i] = [a, b]

    def stage4(i):
        for copy in y_first[i][2:] + y_second[i]:
            copy.wait_recv()
        own = block(0, core * SLOT)

        def total(at):
            cols = pl.ds(at, F)
            return (
                part[i, own, cols]
                + ysecond[i, 0, :, cols].astype(F32)
                + ysecond[i, 1, :, cols].astype(F32)
            )

        ext = pl.ds(3 * F, EXT)
        logit = (
            part[i, own, ext][:, 0:1]
            + decode(ysecond[i, 0, :, ext])
            + decode(ysecond[i, 1, :, ext])
        )
        scale = jax.nn.sigmoid(logit)
        gate, up, raw = total(0), total(F), total(2 * F)
        sig = jax.nn.sigmoid(gate)
        silu = gate * sig
        act = silu * up
        act_grad = scale * raw
        out = block(0, i * CH + core * SLOT)
        gact[out, pl.ds(0, F)] = (act_grad * up * sig * (1.0 + gate * (1.0 - sig))).astype(BF16)
        gact[out, pl.ds(F, F)] = (act_grad * silu).astype(BF16)
        gact[out, pl.ds(2 * F, F)] = (scale * act).astype(BF16)
        dots = jnp.sum(act * raw, axis=1, keepdims=True)
        gact[out, ext] = encode(scale * (1.0 - scale) * dots, OWN)
        g_first[i] = [
            send(gact.at[out], gact.at[out], at_y(1)),
            send(gact.at[out], gact.at[out], at_y(-1)),
        ]

    def stage5(i):
        base = i * CH + core * SLOT
        g_first[i][0].wait_recv()
        left = gact.at[block(-1, base), pl.ds(0, H)]
        a = send(left, left, at_y(1))
        g_first[i][1].wait_recv()
        right = gact.at[block(1, base), pl.ds(H, H)]
        b = send(right, right, at_y(-1))
        g_second[i] = [a, b]

    def stage6(i):
        for copy in g_second[i]:
            copy.wait_recv()
        half = gact.at[pl.ds(pl.multiple_of(i * CH + core * SLOT, SLOT), SLOT)]
        core_back[i] = send(half, half, sibling)

    def stage7(i):
        core_back[i].wait_recv()
        rows = pl.ds(i * CH, CH)

        @pl.loop(0, D // 256)
        def _(t):
            cols = pl.ds(pl.multiple_of(t * 256, 256), 256)
            out = nt(gact[rows, pl.ds(0, 2 * F)], wgu[cols, :])
            for s in range(2):
                for j in range(NX):
                    piece = out[s * SLOT + j * OWN : s * SLOT + (j + 1) * OWN]
                    if j == 0:
                        rgf[i, s, :, cols] = piece
                    else:
                        xsend[i, s, j - 1, :, cols] = piece.astype(BF16)

        for s in range(2):
            for j in range(NX):
                ext = gact[pl.ds(i * CH + s * SLOT + j * OWN, OWN), pl.ds(3 * F, EXT)]
                if j == 0:
                    rgf[i, s, :, pl.ds(D, EXT)] = jnp.broadcast_to(decode(ext), (OWN, EXT))
                else:
                    xsend[i, s, j - 1, :, pl.ds(D, EXT)] = ext
        x_out[i] = [
            send(xsend.at[i, :, j - 1], xrecv.at[i, j - 1], at_x(j)) for j in (2, 1, 3)
        ]

    def stage8(i):
        for copy in x_out[i]:
            copy.wait_recv()
        for s in range(2):
            k = 2 * i + s
            total = rgf[i, s, :, pl.ds(0, D)]
            extra = rgf[i, s, :, pl.ds(D, EXT)][:, 0:1]
            for j in range(NX - 1):
                total = total + xrecv[i, j, s, :, pl.ds(0, D)].astype(F32)
                extra = extra + decode(xrecv[i, j, s, :, pl.ds(D, EXT)])
            if k == 0:
                zown[:, pl.ds(0, D)] = total
                zown[:, pl.ds(D, EXT)] = jnp.broadcast_to(extra, (OWN, EXT))
            else:
                zsend[k - 1, :, pl.ds(0, D)] = total.astype(BF16)
                zsend[k - 1, :, pl.ds(D, EXT)] = encode(extra, OWN)
                z_out[k] = send(zsend.at[k - 1], zrecv.at[k - 1], at_z(OFFSETS[k]))

    for i in range(NCH):
        stage1(i)
        if i >= 1:
            stage5(i - 1)
        stage2(i)
        if i >= 1:
            stage6(i - 1)
        if i >= 2:
            stage8(i - 2)
        stage3(i)
        if i >= 1:
            stage7(i - 1)
        stage4(i)
    stage5(NCH - 1)

    for copy in lg:
        copy.wait_recv()
    logits = lsend[0:1, :]
    for d in range(2 * NY - 1):
        logits = logits + lrecv[d, 0:1, :]
    logit_col = jnp.sum(jnp.where(eye, logits, 0.0), axis=1, keepdims=True)
    eye_half = lax.broadcasted_iota(jnp.int32, (half_tok, half_tok), 0) == (
        lax.broadcasted_iota(jnp.int32, (half_tok, half_tok), 1)
    )
    teacher = jnp.concatenate(
        [
            jnp.sum(jnp.where(eye_half, teacher_ref[s : s + 1, :], 0.0), axis=1, keepdims=True)
            for s in range(2)
        ],
        axis=0,
    )
    token_grad = jax.nn.sigmoid(logit_col) - teacher
    router = jnp.sum(token_grad * hid[...].astype(F32), axis=0, keepdims=True)

    stage6(NCH - 1)
    stage8(NCH - 2)
    stage7(NCH - 1)

    routed = tn(gact[:, pl.ds(3 * F, EXT)], agb[0])
    router = router + routed[0:1] + routed[EXT // 2 : EXT // 2 + 1]
    for a in range(D // 128):
        rparts_x[x, a : a + 1, :] = router[:, a * 128 : (a + 1) * 128]
    rx = [send(rparts_x.at[x], rparts_x.at[x], at_x(d)) for d in range(1, NX)]

    @pl.loop(0, D // 256)
    def _(t):
        cols = pl.ds(pl.multiple_of(t * 256, 256), 256)
        out = tn(agb[0, :, cols], gact[:, pl.ds(0, 2 * F)])
        gg_out[cols, :] = out[:, :F].astype(BF16)
        ug_out[cols, :] = out[:, F:].astype(BF16)

    stores = [local(gg_out, gg_hbm), local(ug_out, ug_hbm)]
    stage8(NCH - 1)

    for copy in rx:
        copy.wait_recv()
    rparts_z[z] = rparts_x[0] + rparts_x[1] + rparts_x[2] + rparts_x[3]
    rz = [send(rparts_z.at[z], rparts_z.at[z], at_z(d)) for d in range(1, NZ)]

    @pl.loop(0, F // 128)
    def _(t):
        cols = pl.ds(pl.multiple_of(t * 128, 128), 128)
        acts = gact[:, pl.ds(pl.multiple_of(2 * F + t * 128, 128), 128)]
        dg_out[cols, :] = tn(acts, agb[1]).astype(BF16)

    stores.append(local(dg_out, dg_hbm))

    for k in range(1, NZ):
        z_out[k].wait_recv()
    total = zown[:, pl.ds(0, D)]
    extra = zown[:, pl.ds(D, EXT)][:, 0:1]
    for k in range(NZ - 1):
        total = total + zrecv[k, :, pl.ds(0, D)].astype(F32)
        extra = extra + decode(zrecv[k, :, pl.ds(D, EXT)])
    total = total + extra * rw_ref[...]
    high = total.astype(BF16)
    low = (total - high.astype(F32)).astype(BF16)
    place16 = place.astype(BF16)
    hg_out[...] = (
        token_grad * rw_ref[...]
        + jnp.dot(place16, high, preferred_element_type=F32)
        + jnp.dot(place16, low, preferred_element_type=F32)
    ).astype(BF16)
    stores.append(local(hg_out, hg_hbm))

    for copy in rz:
        copy.wait_recv()
    final = rparts_z[0]
    for k in range(1, NZ):
        final = final + rparts_z[k]
    for a in range(D // 128):
        rg_ref[:, a * 128 : (a + 1) * 128] = final[a : a + 1, :]

    for copy in started:
        copy.wait_send()
    for copy in stores:
        copy.wait()


def on_device(
    hidden, router_weight, teacher, positions, cotangent, gate_weight, up_weight, down_weight
):
    slabs, rows_dev, D = hidden.shape
    F = gate_weight.shape[1]
    C = 3 * F + EXT
    vmem = pl.BlockSpec(memory_space=pltpu.VMEM)
    smem = pl.BlockSpec(memory_space=pltpu.SMEM)
    hbm = pl.BlockSpec(memory_space=pl.ANY)
    copies = 3 + 8 + 7 + NCH * 15 + 7 + 3 + 7
    hidden_grad, router_grad, gate_grad, up_grad, down_grad = pl.pallas_call(
        functools.partial(kernel, D, F),
        out_shape=(
            jax.ShapeDtypeStruct((TOK, D), BF16),
            jax.ShapeDtypeStruct((1, D), F32),
            jax.ShapeDtypeStruct((D, F), BF16),
            jax.ShapeDtypeStruct((D, F), BF16),
            jax.ShapeDtypeStruct((F, D), BF16),
        ),
        in_specs=[hbm, vmem, vmem, smem, vmem, hbm, hbm, hbm],
        out_specs=(hbm, vmem, hbm, hbm, hbm),
        scratch_shapes=[
            pltpu.VMEM((TOK, D), BF16),
            pltpu.VMEM((D, 2 * F), BF16),
            pltpu.VMEM((F, D), BF16),
            pltpu.VMEM((2, ROWS, D), BF16),
            pltpu.VMEM((NCH, CH, C), F32),
            pltpu.VMEM((NCH, SLOT, C), BF16),
            pltpu.VMEM((NCH, SLOT, C), BF16),
            pltpu.VMEM((NCH, SLOT, C), BF16),
            pltpu.VMEM((NCH, 2, OWN, C // 2), BF16),
            pltpu.VMEM((NCH, 2, OWN, C), BF16),
            pltpu.VMEM((NCH, 2, OWN, C // 2), BF16),
            pltpu.VMEM((ROWS, C), BF16),
            pltpu.VMEM((NCH, 2, OWN, D + EXT), F32),
            pltpu.VMEM((NCH, 2, NX - 1, OWN, D + EXT), BF16),
            pltpu.VMEM((NCH, NX - 1, 2, OWN, D + EXT), BF16),
            pltpu.VMEM((OWN, D + EXT), F32),
            pltpu.VMEM((NZ - 1, OWN, D + EXT), BF16),
            pltpu.VMEM((NZ - 1, OWN, D + EXT), BF16),
            pltpu.VMEM((8, TOK), F32),
            pltpu.VMEM((2 * NY - 1, 8, TOK), F32),
            pltpu.VMEM((NX, D // 128, 128), F32),
            pltpu.VMEM((NZ, D // 128, 128), F32),
            pltpu.VMEM((TOK, D), BF16),
            pltpu.VMEM((D, F), BF16),
            pltpu.VMEM((D, F), BF16),
            pltpu.VMEM((F, D), BF16),
            pltpu.SemaphoreType.DMA((copies,)),
            pltpu.SemaphoreType.DMA((copies,)),
            pltpu.SemaphoreType.DMA((8,)),
        ],
        compiler_params=pltpu.CompilerParams(
            collective_id=0,
            has_side_effects=True,
            vmem_limit_bytes=58 * 1024 * 1024,
        ),
    )(
        hidden.reshape(slabs * rows_dev, D),
        router_weight.reshape(1, D),
        teacher,
        positions,
        cotangent,
        gate_weight,
        up_weight,
        down_weight,
    )
    return (
        hidden_grad.reshape(hidden.shape),
        router_grad.reshape(D),
        gate_grad,
        up_grad,
        down_grad,
    )


def solution(mesh):
    in_specs = (
        P(None, "wide", "narrow"),
        P("narrow"),
        P(None, "wide"),
        P(),
        P(None, "wide", "narrow"),
        P("narrow", "wide"),
        P("narrow", "wide"),
        P("wide", "narrow"),
    )
    out_specs = (
        P(None, "wide", "narrow"),
        P("narrow"),
        P("narrow", "wide"),
        P("narrow", "wide"),
        P("wide", "narrow"),
    )
    return jax.shard_map(
        on_device, mesh=mesh, in_specs=in_specs, out_specs=out_specs, check_vma=False
    )
```

```python
import functools

import jax
import jax.numpy as jnp
from jax import lax
from jax.experimental import pallas as pl
from jax.experimental.pallas import tpu as pltpu
from jax.sharding import PartitionSpec as P

MESH = pl.DeviceIdType.MESH
F32 = jnp.float32
BF16 = jnp.bfloat16

NX, NZ, NY = 4, 8, 4
TOK = 128
OWN = 16
ROWS = OWN * NX * NZ
SLOT = OWN * NX
CH = 2 * SLOT
NCH = ROWS // CH
EXT = 128
OFFSETS = (0, 1, -1, 2, -2, 3, -3, 4)

ORDER = (
    "GR:0", "GC:0", "T:0", "GR:1", "GC:1", "A:0", "GR:2", "B:0",
    "GC:2", "A:1", "GR:3", "D:0", "B:1", "GC:3", "A:2", "B:2",
    "A:3", "E:0", "D:1", "B:3", "F:0", "G:0", "D:2", "E:1",
    "D:3", "H:0", "F:1", "E:2", "G:1", "E:3", "F:2", "G:2",
    "F:3", "G:3", "H:1", "RX:0", "WI:0", "WI:1", "WI:2", "RZ:0",
    "WI:3", "H:2", "WO:0", "WO:1", "WO:2", "WO:3", "H:3",
)


def encode(value, rows):
    wide = jnp.broadcast_to(value, (rows, EXT))
    high = wide.astype(BF16).astype(F32)
    lane = lax.broadcasted_iota(jnp.int32, (rows, EXT), 1)
    return jnp.where(lane < EXT // 2, high, wide - high).astype(BF16)


def decode(block):
    return block[:, 0:1].astype(F32) + block[:, EXT // 2 : EXT // 2 + 1].astype(F32)


def nt(a, b):
    return lax.dot_general(a, b, (((1,), (1,)), ((), ())), preferred_element_type=F32)


def tn(a, b):
    return lax.dot_general(a, b, (((0,), (0,)), ((), ())), preferred_element_type=F32)


def tiles(extent, step):
    return [(at, min(step, extent - at)) for at in range(0, extent, step)]


def kernel(
    D,
    F,
    hidden_hbm,
    rw_ref,
    teacher_ref,
    pos_ref,
    cot_ref,
    gw_hbm,
    uw_hbm,
    dw_hbm,
    hg_out,
    rg_ref,
    gg_out,
    ug_out,
    dg_out,
    hid,
    wgu,
    wd,
    agb,
    part,
    csend,
    crecv,
    ysend,
    yrecv,
    gact,
    rgf,
    xsend,
    xrecv,
    zown,
    zsend,
    zrecv,
    lsend,
    lrecv,
    rparts_x,
    rparts_z,
    tgrad,
    send_sem,
    recv_sem,
    local_sem,
):
    C = 3 * F + EXT
    H = C // 2
    wide, narrow = lax.axis_index("wide"), lax.axis_index("narrow")
    x, z = lax.div(wide, NZ), lax.rem(wide, NZ)
    y, core = lax.div(narrow, 2), lax.rem(narrow, 2)

    def at_x(d):
        return (lax.rem(x + d + NX, NX) * NZ + z, narrow)

    def at_z(d):
        return (x * NZ + lax.rem(z + d + NZ, NZ), narrow)

    def at_y(d):
        return (wide, lax.rem(y + d + NY, NY) * 2 + core)

    def at_n(d):
        return (wide, lax.rem(narrow + d, 2 * NY))

    sibling = (wide, y * 2 + (1 - core))

    count = [0]
    started = []

    def send(src, dst, device):
        i = count[0]
        count[0] += 1
        copy = pltpu.make_async_remote_copy(
            src_ref=src,
            dst_ref=dst,
            send_sem=send_sem.at[i],
            recv_sem=recv_sem.at[i],
            device_id=device,
            device_id_type=MESH,
        )
        copy.start()
        started.append(copy)
        return copy

    lcount = [0]

    def local(src, dst):
        copy = pltpu.make_async_copy(src, dst, local_sem.at[lcount[0]])
        lcount[0] += 1
        copy.start()
        return copy

    load_hid = local(hidden_hbm, hid)
    load_w = [
        local(gw_hbm, wgu.at[:, pl.ds(0, F)]),
        local(uw_hbm, wgu.at[:, pl.ds(F, F)]),
        local(dw_hbm, wd),
    ]

    barrier = pltpu.get_barrier_semaphore()
    peers = (
        [at_x(d) for d in range(1, NX)]
        + [at_z(d) for d in range(1, NZ)]
        + [at_n(d) for d in range(1, 2 * NY)]
    )
    for peer in peers:
        pl.semaphore_signal(barrier, inc=1, device_id=peer, device_id_type=MESH)

    sub = lax.broadcasted_iota(jnp.int32, (OWN, TOK), 0)
    lane = lax.broadcasted_iota(jnp.int32, (OWN, TOK), 1)
    sub_t = lax.broadcasted_iota(jnp.int32, (TOK, OWN), 0)
    lane_t = lax.broadcasted_iota(jnp.int32, (TOK, OWN), 1)
    pick = jnp.zeros((OWN, TOK), F32)
    place = jnp.zeros((TOK, OWN), F32)
    half_own, half_tok = OWN // 2, TOK // 2
    for r in range(OWN):
        s, j = r // half_own, r % half_own
        token = pos_ref[s, wide * half_own + j] - wide * half_tok + s * half_tok
        pick = jnp.where((sub == r) & (lane == token), 1.0, pick)
        place = jnp.where((lane_t == r) & (sub_t == token), 1.0, place)
    load_hid.wait()
    own_rows = jnp.dot(pick.astype(BF16), hid[...], preferred_element_type=F32)
    agb[0, pl.ds(0, OWN), :] = own_rows.astype(BF16)
    agb[1, pl.ds(0, OWN), :] = jnp.concatenate(
        [cot_ref[0].astype(F32), cot_ref[1].astype(F32)], axis=0
    ).astype(BF16)
    pl.semaphore_wait(barrier, len(peers))

    def gather_x(which):
        own = agb.at[which, pl.ds(0, OWN)]
        return [
            send(own, agb.at[which, pl.ds((NX - d) * OWN, OWN)], at_x(d)) for d in (2, 1, 3)
        ]

    gx = {0: gather_x(0)}

    eye = lax.broadcasted_iota(jnp.int32, (TOK, TOK), 0) == lax.broadcasted_iota(
        jnp.int32, (TOK, TOK), 1
    )
    logit_col = jnp.sum(hid[...].astype(F32) * rw_ref[...], axis=1, keepdims=True)
    logit_row = jnp.sum(jnp.where(eye, logit_col, 0.0), axis=0, keepdims=True)
    lsend[...] = jnp.broadcast_to(logit_row, (8, TOK))
    lg = [send(lsend, lrecv.at[d - 1], at_n(d)) for d in range(1, 2 * NY)]

    gz = {}

    def ring(which, src, dst, d, at=0, n=SLOT):
        return send(
            agb.at[which, pl.ds(src * SLOT + at, n)],
            agb.at[which, pl.ds(dst * SLOT + at, n)],
            at_z(d),
        )

    def gather(which, step):
        for copy in gx[which] if step == 0 else gz[which, step]:
            copy.wait_recv()
        if step == 0:
            gz[which, 1] = [ring(which, 0, 1, -1), ring(which, 0, 2, 1)]
            if which == 0:
                gx[1] = gather_x(1)
        elif step == 1:
            gz[which, 2] = [ring(which, 1, 3, -1), ring(which, 2, 4, 1)]
        elif step == 2:
            gz[which, 3] = [ring(which, 3, 5, -1), ring(which, 4, 6, 1)]
        elif step == 3:
            half = SLOT // 2
            gz[which, 4] = [
                ring(which, 5, 7, -1, 0, half),
                ring(which, 6, 7, 1, half, half),
            ]

    core_out, y_out, g_first, g_second, core_back, x_out, z_out = ({} for _ in range(7))

    def block(j, base=0):
        return pl.ds(pl.multiple_of(base + lax.rem(y + j + NY, NY) * OWN, OWN), OWN)

    def stage1(i):
        rows = pl.ds(i * CH, CH)
        if i == 0:
            for copy in load_w:
                copy.wait()
        if i == NCH - 1:
            for which in (0, 1):
                for copy in gz[which, 4]:
                    copy.wait_recv()

        for at, n in tiles(2 * F, 256):
            cols = pl.ds(at, n)
            part[i, :, cols] = jnp.dot(
                agb[0, rows, :], wgu[:, cols], preferred_element_type=F32
            )

        for at, n in tiles(F, 256):
            part[i, :, pl.ds(2 * F + at, n)] = nt(agb[1, rows, :], wd[pl.ds(at, n), :])
        logit = jnp.sum(agb[0, rows, :].astype(F32) * rw_ref[...], axis=1, keepdims=True)
        part[i, :, pl.ds(3 * F, EXT)] = jnp.broadcast_to(logit, (CH, EXT))
        other = pl.ds(pl.multiple_of((1 - core) * SLOT, SLOT), SLOT)
        csend[i, :, pl.ds(0, 3 * F)] = part[i, other, pl.ds(0, 3 * F)].astype(BF16)
        csend[i, :, pl.ds(3 * F, EXT)] = encode(
            part[i, other, pl.ds(3 * F, EXT)][:, 0:1], SLOT
        )
        core_out[i] = send(csend.at[i], crecv.at[i], sibling)

    def stage2(i):
        core_out[i].wait_recv()
        base = pl.multiple_of(core * SLOT, SLOT)
        mine = pl.ds(base, SLOT)
        total = part[i, mine, pl.ds(0, 3 * F)] + crecv[i, :, pl.ds(0, 3 * F)].astype(F32)
        part[i, mine, pl.ds(0, 3 * F)] = total
        ysend[i, :, pl.ds(0, 3 * F)] = total.astype(BF16)
        logit = part[i, mine, pl.ds(3 * F, EXT)][:, 0:1] + decode(
            crecv[i, :, pl.ds(3 * F, EXT)]
        )
        part[i, mine, pl.ds(3 * F, EXT)] = jnp.broadcast_to(logit, (SLOT, EXT))
        ysend[i, :, pl.ds(3 * F, EXT)] = encode(logit, SLOT)
        y_out[i] = [
            send(ysend.at[i, block(d)], yrecv.at[i, d - 1], at_y(d)) for d in (2, 1, 3)
        ]

    def stage4(i):
        for copy in y_out[i]:
            copy.wait_recv()
        own = block(0, core * SLOT)

        def total(at):
            cols = pl.ds(at, F)
            value = part[i, own, cols]
            for d in range(NY - 1):
                value = value + yrecv[i, d, :, cols].astype(F32)
            return value

        ext = pl.ds(3 * F, EXT)
        logit = part[i, own, ext][:, 0:1]
        for d in range(NY - 1):
            logit = logit + decode(yrecv[i, d, :, ext])
        scale = jax.nn.sigmoid(logit)
        gate, up, raw = total(0), total(F), total(2 * F)
        sig = jax.nn.sigmoid(gate)
        silu = gate * sig
        act = silu * up
        act_grad = scale * raw
        out = block(0, i * CH + core * SLOT)
        gact[out, pl.ds(0, F)] = (act_grad * up * sig * (1.0 + gate * (1.0 - sig))).astype(BF16)
        gact[out, pl.ds(F, F)] = (act_grad * silu).astype(BF16)
        gact[out, pl.ds(2 * F, F)] = (scale * act).astype(BF16)
        dots = jnp.sum(act * raw, axis=1, keepdims=True)
        gact[out, ext] = encode(scale * (1.0 - scale) * dots, OWN)
        g_first[i] = [
            send(gact.at[out], gact.at[out], at_y(1)),
            send(gact.at[out], gact.at[out], at_y(-1)),
        ]

    def stage5(i):
        base = i * CH + core * SLOT
        g_first[i][0].wait_recv()
        left = gact.at[block(-1, base), pl.ds(0, H)]
        a = send(left, left, at_y(1))
        g_first[i][1].wait_recv()
        right = gact.at[block(1, base), pl.ds(H, H)]
        b = send(right, right, at_y(-1))
        g_second[i] = [a, b]

    def stage6(i):
        for copy in g_second[i]:
            copy.wait_recv()
        half = gact.at[pl.ds(pl.multiple_of(i * CH + core * SLOT, SLOT), SLOT)]
        core_back[i] = send(half, half, sibling)

    def stage7(i):
        core_back[i].wait_recv()
        rows = pl.ds(i * CH, CH)

        for at, n in tiles(D, 256):
            cols = pl.ds(at, n)
            out = nt(gact[rows, pl.ds(0, 2 * F)], wgu[cols, :])
            for s in range(2):
                for j in range(NX):
                    piece = out[s * SLOT + j * OWN : s * SLOT + (j + 1) * OWN]
                    if j == 0:
                        rgf[i, s, :, cols] = piece
                    else:
                        xsend[i, s, j - 1, :, cols] = piece.astype(BF16)

        for s in range(2):
            for j in range(NX):
                ext = gact[pl.ds(i * CH + s * SLOT + j * OWN, OWN), pl.ds(3 * F, EXT)]
                if j == 0:
                    rgf[i, s, :, pl.ds(D, EXT)] = jnp.broadcast_to(decode(ext), (OWN, EXT))
                else:
                    xsend[i, s, j - 1, :, pl.ds(D, EXT)] = ext
        x_out[i] = [
            send(xsend.at[i, :, j - 1], xrecv.at[i, j - 1], at_x(j)) for j in (2, 1, 3)
        ]

    def stage8(i):
        for copy in x_out[i]:
            copy.wait_recv()
        for s in range(2):
            k = 2 * i + s
            total = rgf[i, s, :, pl.ds(0, D)]
            extra = rgf[i, s, :, pl.ds(D, EXT)][:, 0:1]
            for j in range(NX - 1):
                total = total + xrecv[i, j, s, :, pl.ds(0, D)].astype(F32)
                extra = extra + decode(xrecv[i, j, s, :, pl.ds(D, EXT)])
            if k == 0:
                zown[:, pl.ds(0, D)] = total
                zown[:, pl.ds(D, EXT)] = jnp.broadcast_to(extra, (OWN, EXT))
            else:
                zsend[k - 1, :, pl.ds(0, D)] = total.astype(BF16)
                zsend[k - 1, :, pl.ds(D, EXT)] = encode(extra, OWN)
                z_out[k] = send(zsend.at[k - 1], zrecv.at[k - 1], at_z(OFFSETS[k]))

    held = {}

    def own_tokens():
        for copy in lg:
            copy.wait_recv()
        logits = lsend[0:1, :]
        for d in range(2 * NY - 1):
            logits = logits + lrecv[d, 0:1, :]
        logit_col = jnp.sum(jnp.where(eye, logits, 0.0), axis=1, keepdims=True)
        eye_half = lax.broadcasted_iota(jnp.int32, (half_tok, half_tok), 0) == (
            lax.broadcasted_iota(jnp.int32, (half_tok, half_tok), 1)
        )
        teacher = jnp.concatenate(
            [
                jnp.sum(jnp.where(eye_half, teacher_ref[s : s + 1, :], 0.0), axis=1, keepdims=True)
                for s in range(2)
            ],
            axis=0,
        )
        grad = jax.nn.sigmoid(logit_col) - teacher
        router = jnp.sum(grad * hid[...].astype(F32), axis=0, keepdims=True)
        for a in range(D // 128):
            rparts_x[x, a : a + 1, :] = router[:, a * 128 : (a + 1) * 128]
        tgrad[...] = jnp.broadcast_to(grad, (TOK, 128))

    def router_x():
        routed = tn(gact[:, pl.ds(3 * F, EXT)], agb[0])
        routed = routed[0:1] + routed[EXT // 2 : EXT // 2 + 1]
        for a in range(D // 128):
            rparts_x[x, a : a + 1, :] += routed[:, a * 128 : (a + 1) * 128]
        held["rx"] = [send(rparts_x.at[x], rparts_x.at[x], at_x(d)) for d in range(1, NX)]

    def router_z():
        for copy in held["rx"]:
            copy.wait_recv()
        rparts_z[z] = rparts_x[0] + rparts_x[1] + rparts_x[2] + rparts_x[3]
        held["rz"] = [send(rparts_z.at[z], rparts_z.at[z], at_z(d)) for d in range(1, NZ)]

    def grads_in(t):
        cols = pl.ds(t * 256, 256)
        out = tn(agb[0, :, cols], gact[:, pl.ds(0, 2 * F)])
        gg_out[cols, :] = out[:, :F].astype(BF16)
        ug_out[cols, :] = out[:, F:].astype(BF16)

    def grads_out(t):
        at, n = tiles(F, 256)[t]
        dg_out[pl.ds(at, n), :] = tn(gact[:, pl.ds(2 * F + at, n)], agb[1]).astype(BF16)

    tasks = {
        "GR": lambda step: gather(0, step),
        "GC": lambda step: gather(1, step),
        "A": stage1,
        "B": stage2,
        "D": stage4,
        "E": stage5,
        "F": stage6,
        "G": stage7,
        "H": stage8,
        "T": lambda _: own_tokens(),
        "RX": lambda _: router_x(),
        "RZ": lambda _: router_z(),
        "WI": grads_in,
        "WO": grads_out,
    }
    for task in ORDER:
        name, step = task.split(":")
        tasks[name](int(step))

    for k in range(1, NZ):
        z_out[k].wait_recv()
    total = zown[:, pl.ds(0, D)]
    extra = zown[:, pl.ds(D, EXT)][:, 0:1]
    for k in range(NZ - 1):
        total = total + zrecv[k, :, pl.ds(0, D)].astype(F32)
        extra = extra + decode(zrecv[k, :, pl.ds(D, EXT)])
    total = total + extra * rw_ref[...]
    high = total.astype(BF16)
    low = (total - high.astype(F32)).astype(BF16)
    place16 = place.astype(BF16)
    hg_out[...] = (
        tgrad[:, 0:1] * rw_ref[...]
        + jnp.dot(place16, high, preferred_element_type=F32)
        + jnp.dot(place16, low, preferred_element_type=F32)
    ).astype(BF16)

    for copy in held["rz"]:
        copy.wait_recv()
    final = rparts_z[0]
    for k in range(1, NZ):
        final = final + rparts_z[k]
    for a in range(D // 128):
        rg_ref[:, a * 128 : (a + 1) * 128] = final[a : a + 1, :]

    for copy in started:
        copy.wait_send()


def on_device(
    hidden, router_weight, teacher, positions, cotangent, gate_weight, up_weight, down_weight
):
    slabs, rows_dev, D = hidden.shape
    F = gate_weight.shape[1]
    C = 3 * F + EXT
    vmem = pl.BlockSpec(memory_space=pltpu.VMEM)
    smem = pl.BlockSpec(memory_space=pltpu.SMEM)
    hbm = pl.BlockSpec(memory_space=pl.ANY)
    copies = 6 + 16 + 7 + NCH * 12 + 7 + 3 + 7
    hidden_grad, router_grad, gate_grad, up_grad, down_grad = pl.pallas_call(
        functools.partial(kernel, D, F),
        out_shape=(
            pltpu.VMEM((TOK, D), BF16),
            pltpu.VMEM((1, D), F32),
            pltpu.VMEM((D, F), BF16),
            pltpu.VMEM((D, F), BF16),
            pltpu.VMEM((F, D), BF16),
        ),
        in_specs=[hbm, vmem, vmem, smem, vmem, hbm, hbm, hbm],
        out_specs=(vmem,)*5,
        scratch_shapes=[
            pltpu.VMEM((TOK, D), BF16),
            pltpu.VMEM((D, 2 * F), BF16),
            pltpu.VMEM((F, D), BF16),
            pltpu.VMEM((2, ROWS, D), BF16),
            pltpu.VMEM((NCH, CH, C), F32),
            pltpu.VMEM((NCH, SLOT, C), BF16),
            pltpu.VMEM((NCH, SLOT, C), BF16),
            pltpu.VMEM((NCH, SLOT, C), BF16),
            pltpu.VMEM((NCH, NY - 1, OWN, C), BF16),
            pltpu.VMEM((ROWS, C), BF16),
            pltpu.VMEM((NCH, 2, OWN, D + EXT), F32),
            pltpu.VMEM((NCH, 2, NX - 1, OWN, D + EXT), BF16),
            pltpu.VMEM((NCH, NX - 1, 2, OWN, D + EXT), BF16),
            pltpu.VMEM((OWN, D + EXT), F32),
            pltpu.VMEM((NZ - 1, OWN, D + EXT), BF16),
            pltpu.VMEM((NZ - 1, OWN, D + EXT), BF16),
            pltpu.VMEM((8, TOK), F32),
            pltpu.VMEM((2 * NY - 1, 8, TOK), F32),
            pltpu.VMEM((NX, D // 128, 128), F32),
            pltpu.VMEM((NZ, D // 128, 128), F32),
            pltpu.VMEM((TOK, 128), F32),
            pltpu.SemaphoreType.DMA((copies,)),
            pltpu.SemaphoreType.DMA((copies,)),
            pltpu.SemaphoreType.DMA((8,)),
        ],
        compiler_params=pltpu.CompilerParams(
            collective_id=0,
            has_side_effects=True,
            vmem_limit_bytes=58 * 1024 * 1024,
        ),
    )(
        hidden.reshape(slabs * rows_dev, D),
        router_weight.reshape(1, D),
        teacher,
        positions,
        cotangent,
        gate_weight,
        up_weight,
        down_weight,
    )
    return (
        hidden_grad.reshape(hidden.shape),
        router_grad.reshape(D),
        gate_grad,
        up_grad,
        down_grad,
    )


def solution(mesh):
    in_specs = (
        P(None, "wide", "narrow"),
        P("narrow"),
        P(None, "wide"),
        P(),
        P(None, "wide", "narrow"),
        P("narrow", "wide"),
        P("narrow", "wide"),
        P("wide", "narrow"),
    )
    out_specs = (
        P(None, "wide", "narrow"),
        P("narrow"),
        P("narrow", "wide"),
        P("narrow", "wide"),
        P("wide", "narrow"),
    )
    return jax.shard_map(
        on_device, mesh=mesh, in_specs=in_specs, out_specs=out_specs, check_vma=False
    )
```

```python
import functools

import jax
import jax.numpy as jnp
from jax import lax
from jax.experimental import pallas as pl
from jax.experimental.pallas import tpu as pltpu
from jax.sharding import PartitionSpec as P

MESH = pl.DeviceIdType.MESH
F32 = jnp.float32
BF16 = jnp.bfloat16

NX, NZ, NY = 4, 8, 4
TOK = 128
OWN = 16
ROWS = OWN * NX * NZ
SLOT = OWN * NX
CHUNKS = ((0,), (1, 2), (3, 4), (5, 6), (7,))
NCH = len(CHUNKS)
KEEPER = {0: 0, NCH - 1: 1}
EXT = 128
OFFSETS = (0, 1, -1, 2, -2, 3, -3, 4)

ORDER = (
    "GR:0", "GC:0", "A:0", "T:0", "B:0", "GR:1", "GC:1", "A:1",
    "D:0", "B:1", "E:0", "GR:2", "GC:2", "A:2", "F:0", "D:1",
    "B:2", "G:0", "GR:3", "GC:3", "A:3", "H:0", "E:1", "B:3",
    "A:4", "D:2", "F:1", "B:4", "G:1", "D:3", "E:2", "D:4",
    "H:1", "F:2", "E:4", "E:3", "G:2", "F:4", "F:3", "G:4",
    "G:3", "RX:0", "H:2", "WI:0", "WI:1", "WI:2", "H:4", "RZ:0",
    "WI:3", "WO:0", "WO:1", "WO:2", "WO:3", "H:3",
)


def encode(value, rows):
    wide = jnp.broadcast_to(value, (rows, EXT))
    high = wide.astype(BF16).astype(F32)
    lane = lax.broadcasted_iota(jnp.int32, (rows, EXT), 1)
    return jnp.where(lane < EXT // 2, high, wide - high).astype(BF16)


def decode(block):
    return block[:, 0:1].astype(F32) + block[:, EXT // 2 : EXT // 2 + 1].astype(F32)


def nt(a, b):
    return lax.dot_general(a, b, (((1,), (1,)), ((), ())), preferred_element_type=F32)


def tn(a, b):
    return lax.dot_general(a, b, (((0,), (0,)), ((), ())), preferred_element_type=F32)


def tiles(extent, step):
    return [(at, min(step, extent - at)) for at in range(0, extent, step)]


def kernel(
    D,
    F,
    hidden_hbm,
    rw_ref,
    teacher_ref,
    pos_ref,
    cot_ref,
    gw_hbm,
    uw_hbm,
    dw_hbm,
    hg_out,
    rg_ref,
    gg_out,
    ug_out,
    dg_out,
    hid,
    wgu,
    wd,
    agb,
    part,
    csend,
    crecv,
    ysend,
    yrecv,
    gact,
    rgf,
    xsend,
    xrecv,
    zown,
    zsend,
    zrecv,
    lsend,
    lrecv,
    rparts_x,
    rparts_z,
    tgrad,
    send_sem,
    recv_sem,
    local_sem,
):
    C = 3 * F + EXT
    H = C // 2
    wide, narrow = lax.axis_index("wide"), lax.axis_index("narrow")
    x, z = lax.div(wide, NZ), lax.rem(wide, NZ)
    y, core = lax.div(narrow, 2), lax.rem(narrow, 2)

    def at_x(d):
        return (lax.rem(x + d + NX, NX) * NZ + z, narrow)

    def at_z(d):
        return (x * NZ + lax.rem(z + d + NZ, NZ), narrow)

    def at_y(d):
        return (wide, lax.rem(y + d + NY, NY) * 2 + core)

    def at_n(d):
        return (wide, lax.rem(narrow + d, 2 * NY))

    sibling = (wide, y * 2 + (1 - core))

    count = [0]
    started = []

    def make(src, dst, device):
        i = count[0]
        count[0] += 1
        return pltpu.make_async_remote_copy(
            src_ref=src,
            dst_ref=dst,
            send_sem=send_sem.at[i],
            recv_sem=recv_sem.at[i],
            device_id=device,
            device_id_type=MESH,
        )

    def send(src, dst, device):
        copy = make(src, dst, device)
        copy.start()
        started.append(copy)
        return copy

    def on(core_of_chip, part):
        if core_of_chip is None:
            part()
        else:
            pl.when(core == core_of_chip)(part)

    lcount = [0]

    def local(src, dst):
        copy = pltpu.make_async_copy(src, dst, local_sem.at[lcount[0]])
        lcount[0] += 1
        copy.start()
        return copy

    load_hid = local(hidden_hbm, hid)
    load_w = [
        local(gw_hbm, wgu.at[:, pl.ds(0, F)]),
        local(uw_hbm, wgu.at[:, pl.ds(F, F)]),
        local(dw_hbm, wd),
    ]

    barrier = pltpu.get_barrier_semaphore()
    peers = (
        [at_x(d) for d in range(1, NX)]
        + [at_z(d) for d in range(1, NZ)]
        + [at_n(d) for d in range(1, 2 * NY)]
    )
    for peer in peers:
        pl.semaphore_signal(barrier, inc=1, device_id=peer, device_id_type=MESH)

    sub = lax.broadcasted_iota(jnp.int32, (OWN, TOK), 0)
    lane = lax.broadcasted_iota(jnp.int32, (OWN, TOK), 1)
    sub_t = lax.broadcasted_iota(jnp.int32, (TOK, OWN), 0)
    lane_t = lax.broadcasted_iota(jnp.int32, (TOK, OWN), 1)
    pick = jnp.zeros((OWN, TOK), F32)
    place = jnp.zeros((TOK, OWN), F32)
    half_own, half_tok = OWN // 2, TOK // 2
    for r in range(OWN):
        s, j = r // half_own, r % half_own
        token = pos_ref[s, wide * half_own + j] - wide * half_tok + s * half_tok
        pick = jnp.where((sub == r) & (lane == token), 1.0, pick)
        place = jnp.where((lane_t == r) & (sub_t == token), 1.0, place)
    load_hid.wait()
    own_rows = jnp.dot(pick.astype(BF16), hid[...], preferred_element_type=F32)
    agb[0, pl.ds(0, OWN), :] = own_rows.astype(BF16)
    agb[1, pl.ds(0, OWN), :] = jnp.concatenate(
        [cot_ref[0].astype(F32), cot_ref[1].astype(F32)], axis=0
    ).astype(BF16)
    pl.semaphore_wait(barrier, len(peers))

    def gather_x(which):
        own = agb.at[which, pl.ds(0, OWN)]
        return [
            send(own, agb.at[which, pl.ds((NX - d) * OWN, OWN)], at_x(d)) for d in (2, 1, 3)
        ]

    gx = {0: gather_x(0)}

    eye = lax.broadcasted_iota(jnp.int32, (TOK, TOK), 0) == lax.broadcasted_iota(
        jnp.int32, (TOK, TOK), 1
    )
    logit_col = jnp.sum(hid[...].astype(F32) * rw_ref[...], axis=1, keepdims=True)
    logit_row = jnp.sum(jnp.where(eye, logit_col, 0.0), axis=0, keepdims=True)
    lsend[...] = jnp.broadcast_to(logit_row, (8, TOK))
    gx[1] = gather_x(1)
    lg = [send(lsend, lrecv.at[d - 1], at_n(d)) for d in range(1, 2 * NY)]

    gz = {}

    def ring(which, src, dst, d, at=0, n=SLOT):
        return send(
            agb.at[which, pl.ds(src * SLOT + at, n)],
            agb.at[which, pl.ds(dst * SLOT + at, n)],
            at_z(d),
        )

    def gather(which, step):
        for copy in gx[which] if step == 0 else gz[which, step]:
            copy.wait_recv()
        if step == 0:
            gz[which, 1] = [ring(which, 0, 1, -1), ring(which, 0, 2, 1)]
        elif step == 1:
            gz[which, 2] = [ring(which, 1, 3, -1), ring(which, 2, 4, 1)]
        elif step == 2:
            gz[which, 3] = [ring(which, 3, 5, -1), ring(which, 4, 6, 1)]
        elif step == 3:
            half = SLOT // 2
            gz[which, 4] = [
                ring(which, 5, 7, -1, 0, half),
                ring(which, 6, 7, 1, half, half),
            ]

    core_out, y_out, g_first, g_second, core_back, x_out, z_out = ({} for _ in range(7))

    def block(j, base=0):
        return pl.ds(pl.multiple_of(base + lax.rem(y + j + NY, NY) * OWN, OWN), OWN)

    def chunk(i):
        base, rows = CHUNKS[i][0] * SLOT, len(CHUNKS[i]) * SLOT
        keeper = KEEPER.get(i)
        share = base if keeper is not None else base + core * SLOT
        return keeper, base, rows, share

    def stage1(i):
        keeper, base, n, _ = chunk(i)
        rows = pl.ds(base, n)
        if i == 0:
            for copy in load_w:
                copy.wait()
        if i == NCH - 1:
            for which in (0, 1):
                for copy in gz[which, 4]:
                    copy.wait_recv()
        for at, m in tiles(2 * F, 256):
            cols = pl.ds(at, m)
            part[rows, cols] = jnp.dot(
                agb[0, rows, :], wgu[:, cols], preferred_element_type=F32
            )
        for at, m in tiles(F, 256):
            part[rows, pl.ds(2 * F + at, m)] = nt(agb[1, rows, :], wd[pl.ds(at, m), :])
        logit = jnp.sum(agb[0, rows, :].astype(F32) * rw_ref[...], axis=1, keepdims=True)
        part[rows, pl.ds(3 * F, EXT)] = jnp.broadcast_to(logit, (n, EXT))
        if keeper is None:
            other = pl.ds(pl.multiple_of(base + (1 - core) * SLOT, SLOT), SLOT)
        else:
            other = rows
        copy = make(csend.at[i], crecv.at[i], sibling)
        core_out[i] = copy

        def to_other():
            csend[i, :, pl.ds(0, 3 * F)] = part[other, pl.ds(0, 3 * F)].astype(BF16)
            csend[i, :, pl.ds(3 * F, EXT)] = encode(
                part[other, pl.ds(3 * F, EXT)][:, 0:1], SLOT
            )
            copy.start()

        on(None if keeper is None else 1 - keeper, to_other)

    def stage2(i):
        keeper, _, _, share = chunk(i)
        mine = pl.ds(share if keeper is not None else pl.multiple_of(share, SLOT), SLOT)
        copies = [
            make(ysend.at[i, block(d)], yrecv.at[i, d - 1], at_y(d)) for d in (2, 1, 3)
        ]
        y_out[i] = copies

        def add():
            core_out[i].wait_recv()
            total = part[mine, pl.ds(0, 3 * F)] + crecv[i, :, pl.ds(0, 3 * F)].astype(F32)
            part[mine, pl.ds(0, 3 * F)] = total
            ysend[i, :, pl.ds(0, 3 * F)] = total.astype(BF16)
            logit = part[mine, pl.ds(3 * F, EXT)][:, 0:1] + decode(
                crecv[i, :, pl.ds(3 * F, EXT)]
            )
            part[mine, pl.ds(3 * F, EXT)] = jnp.broadcast_to(logit, (SLOT, EXT))
            ysend[i, :, pl.ds(3 * F, EXT)] = encode(logit, SLOT)
            for copy in copies:
                copy.start()

        on(keeper, add)

    def stage4(i):
        keeper, _, _, share = chunk(i)
        own = block(0, share)
        ext = pl.ds(3 * F, EXT)
        copies = [make(gact.at[own], gact.at[own], at_y(d)) for d in (1, -1)]
        g_first[i] = copies

        def gate_block():
            for copy in y_out[i]:
                copy.wait_recv()

            def total(at):
                cols = pl.ds(at, F)
                value = part[own, cols]
                for d in range(NY - 1):
                    value = value + yrecv[i, d, :, cols].astype(F32)
                return value

            logit = part[own, ext][:, 0:1]
            for d in range(NY - 1):
                logit = logit + decode(yrecv[i, d, :, ext])
            scale = jax.nn.sigmoid(logit)
            gate, up, raw = total(0), total(F), total(2 * F)
            sig = jax.nn.sigmoid(gate)
            silu = gate * sig
            act = silu * up
            act_grad = scale * raw
            gate_pre = act_grad * up * sig * (1.0 + gate * (1.0 - sig))
            gact[own, pl.ds(0, F)] = gate_pre.astype(BF16)
            gact[own, pl.ds(F, F)] = (act_grad * silu).astype(BF16)
            gact[own, pl.ds(2 * F, F)] = (scale * act).astype(BF16)
            dots = jnp.sum(act * raw, axis=1, keepdims=True)
            gact[own, ext] = encode(scale * (1.0 - scale) * dots, OWN)
            for copy in copies:
                copy.start()

        on(keeper, gate_block)

    def stage5(i):
        keeper, _, _, share = chunk(i)
        left = gact.at[block(-1, share), pl.ds(0, H)]
        right = gact.at[block(1, share), pl.ds(H, H)]
        copies = [make(left, left, at_y(1)), make(right, right, at_y(-1))]
        g_second[i] = copies

        def hand_on():
            for first, second in zip(g_first[i], copies):
                first.wait_recv()
                second.start()

        on(keeper, hand_on)

    def stage6(i):
        keeper, _, _, share = chunk(i)
        start = share if keeper is not None else pl.multiple_of(share, SLOT)
        half = gact.at[pl.ds(start, SLOT)]
        copy = make(half, half, sibling)
        core_back[i] = copy

        def give():
            for second in g_second[i]:
                second.wait_recv()
            copy.start()

        on(keeper, give)

    def stage7(i):
        keeper, base, n, _ = chunk(i)
        on(None if keeper is None else 1 - keeper, core_back[i].wait_recv)
        rows = pl.ds(base, n)
        routed = decode(gact[rows, pl.ds(3 * F, EXT)])
        for at, m in tiles(D, 256):
            cols = pl.ds(at, m)
            out = nt(gact[rows, pl.ds(0, 2 * F)], wgu[cols, :]) + routed * rw_ref[:, cols]
            for s, k in enumerate(CHUNKS[i]):
                for j in range(NX):
                    piece = out[s * SLOT + j * OWN : s * SLOT + (j + 1) * OWN]
                    if j == 0:
                        rgf[k, :, cols] = piece
                    else:
                        xsend[k, j - 1, :, cols] = piece.astype(BF16)
        slots = pl.ds(CHUNKS[i][0], len(CHUNKS[i]))
        x_out[i] = [
            send(xsend.at[slots, j - 1], xrecv.at[slots, j - 1], at_x(j)) for j in (2, 1, 3)
        ]

    def stage8(i):
        for copy in x_out[i]:
            copy.wait_recv()
        for k in CHUNKS[i]:
            total = rgf[k]
            for j in range(NX - 1):
                total = total + xrecv[k, j].astype(F32)
            if k == 0:
                zown[...] = total
            else:
                zsend[k - 1] = total.astype(BF16)
                z_out[k] = send(zsend.at[k - 1], zrecv.at[k - 1], at_z(OFFSETS[k]))

    held = {}

    def own_tokens():
        for copy in lg:
            copy.wait_recv()
        logits = lsend[0:1, :]
        for d in range(2 * NY - 1):
            logits = logits + lrecv[d, 0:1, :]
        logit_col = jnp.sum(jnp.where(eye, logits, 0.0), axis=1, keepdims=True)
        eye_half = lax.broadcasted_iota(jnp.int32, (half_tok, half_tok), 0) == (
            lax.broadcasted_iota(jnp.int32, (half_tok, half_tok), 1)
        )
        teacher = jnp.concatenate(
            [
                jnp.sum(jnp.where(eye_half, teacher_ref[s : s + 1, :], 0.0), axis=1, keepdims=True)
                for s in range(2)
            ],
            axis=0,
        )
        grad = jax.nn.sigmoid(logit_col) - teacher
        router = jnp.sum(grad * hid[...].astype(F32), axis=0, keepdims=True)
        for a in range(D // 128):
            rparts_x[x, a : a + 1, :] = router[:, a * 128 : (a + 1) * 128]
        tgrad[...] = jnp.broadcast_to(grad, (TOK, 128))

    def router_x():
        routed = tn(gact[:, pl.ds(3 * F, EXT)], agb[0])
        routed = routed[0:1] + routed[EXT // 2 : EXT // 2 + 1]
        for a in range(D // 128):
            rparts_x[x, a : a + 1, :] += routed[:, a * 128 : (a + 1) * 128]
        held["rx"] = [send(rparts_x.at[x], rparts_x.at[x], at_x(d)) for d in range(1, NX)]

    def router_z():
        for copy in held["rx"]:
            copy.wait_recv()
        rparts_z[z] = rparts_x[0] + rparts_x[1] + rparts_x[2] + rparts_x[3]
        held["rz"] = [send(rparts_z.at[z], rparts_z.at[z], at_z(d)) for d in range(1, NZ)]

    def grads_in(t):
        cols = pl.ds(t * 256, 256)
        out = tn(agb[0, :, cols], gact[:, pl.ds(0, 2 * F)])
        gg_out[cols, :] = out[:, :F].astype(BF16)
        ug_out[cols, :] = out[:, F:].astype(BF16)

    def grads_out(t):
        at, n = tiles(F, 256)[t]
        dg_out[pl.ds(at, n), :] = tn(gact[:, pl.ds(2 * F + at, n)], agb[1]).astype(BF16)

    tasks = {
        "GR": lambda step: gather(0, step),
        "GC": lambda step: gather(1, step),
        "A": stage1,
        "B": stage2,
        "D": stage4,
        "E": stage5,
        "F": stage6,
        "G": stage7,
        "H": stage8,
        "T": lambda _: own_tokens(),
        "RX": lambda _: router_x(),
        "RZ": lambda _: router_z(),
        "WI": grads_in,
        "WO": grads_out,
    }
    for task in ORDER:
        name, step = task.split(":")
        tasks[name](int(step))

    late = list(z_out.values()) + held["rz"]
    late_ids = [id(copy) for copy in late]
    for copy in started:
        if id(copy) not in late_ids:
            copy.wait_send()
    for i in range(NCH):
        keeper = KEEPER.get(i)

        def sent(keeper=keeper, i=i):
            for copy in y_out[i] + g_first[i] + g_second[i] + [core_back[i]]:
                copy.wait_send()

        on(keeper, sent)
        on(None if keeper is None else 1 - keeper, core_out[i].wait_send)

    for k in range(1, NZ):
        z_out[k].wait_recv()
    total = zown[...]
    for k in range(NZ - 1):
        total = total + zrecv[k].astype(F32)
    high = total.astype(BF16)
    low = (total - high.astype(F32)).astype(BF16)
    place16 = place.astype(BF16)
    hg_out[...] = (
        tgrad[:, 0:1] * rw_ref[...]
        + jnp.dot(place16, high, preferred_element_type=F32)
        + jnp.dot(place16, low, preferred_element_type=F32)
    ).astype(BF16)

    for copy in held["rz"]:
        copy.wait_recv()
    final = rparts_z[0]
    for k in range(1, NZ):
        final = final + rparts_z[k]
    for a in range(D // 128):
        rg_ref[:, a * 128 : (a + 1) * 128] = final[a : a + 1, :]

    for copy in late:
        copy.wait_send()


def on_device(
    hidden, router_weight, teacher, positions, cotangent, gate_weight, up_weight, down_weight
):
    slabs, rows_dev, D = hidden.shape
    F = gate_weight.shape[1]
    C = 3 * F + EXT
    vmem = pl.BlockSpec(memory_space=pltpu.VMEM)
    smem = pl.BlockSpec(memory_space=pltpu.SMEM)
    hbm = pl.BlockSpec(memory_space=pl.ANY)
    copies = 6 + 16 + 7 + NCH * 12 + 7 + 3 + 7
    hidden_grad, router_grad, gate_grad, up_grad, down_grad = pl.pallas_call(
        functools.partial(kernel, D, F),
        out_shape=(
            pltpu.VMEM((TOK, D), BF16),
            pltpu.VMEM((1, D), F32),
            pltpu.VMEM((D, F), BF16),
            pltpu.VMEM((D, F), BF16),
            pltpu.VMEM((F, D), BF16),
        ),
        in_specs=[hbm, vmem, vmem, smem, vmem, hbm, hbm, hbm],
        out_specs=(vmem,)*5,
        scratch_shapes=[
            pltpu.VMEM((TOK, D), BF16),
            pltpu.VMEM((D, 2 * F), BF16),
            pltpu.VMEM((F, D), BF16),
            pltpu.VMEM((2, ROWS, D), BF16),
            pltpu.VMEM((ROWS, C), F32),
            pltpu.VMEM((NCH, SLOT, C), BF16),
            pltpu.VMEM((NCH, SLOT, C), BF16),
            pltpu.VMEM((NCH, SLOT, C), BF16),
            pltpu.VMEM((NCH, NY - 1, OWN, C), BF16),
            pltpu.VMEM((ROWS, C), BF16),
            pltpu.VMEM((NZ, OWN, D), F32),
            pltpu.VMEM((NZ, NX - 1, OWN, D), BF16),
            pltpu.VMEM((NZ, NX - 1, OWN, D), BF16),
            pltpu.VMEM((OWN, D), F32),
            pltpu.VMEM((NZ - 1, OWN, D), BF16),
            pltpu.VMEM((NZ - 1, OWN, D), BF16),
            pltpu.VMEM((8, TOK), F32),
            pltpu.VMEM((2 * NY - 1, 8, TOK), F32),
            pltpu.VMEM((NX, D // 128, 128), F32),
            pltpu.VMEM((NZ, D // 128, 128), F32),
            pltpu.VMEM((TOK, 128), F32),
            pltpu.SemaphoreType.DMA((copies,)),
            pltpu.SemaphoreType.DMA((copies,)),
            pltpu.SemaphoreType.DMA((8,)),
        ],
        compiler_params=pltpu.CompilerParams(
            collective_id=0,
            has_side_effects=True,
            vmem_limit_bytes=58 * 1024 * 1024,
        ),
    )(
        hidden.reshape(slabs * rows_dev, D),
        router_weight.reshape(1, D),
        teacher,
        positions,
        cotangent,
        gate_weight,
        up_weight,
        down_weight,
    )
    return (
        hidden_grad.reshape(hidden.shape),
        router_grad.reshape(D),
        gate_grad,
        up_grad,
        down_grad,
    )


def solution(mesh):
    in_specs = (
        P(None, "wide", "narrow"),
        P("narrow"),
        P(None, "wide"),
        P(),
        P(None, "wide", "narrow"),
        P("narrow", "wide"),
        P("narrow", "wide"),
        P("wide", "narrow"),
    )
    out_specs = (
        P(None, "wide", "narrow"),
        P("narrow"),
        P("narrow", "wide"),
        P("narrow", "wide"),
        P("wide", "narrow"),
    )
    return jax.shard_map(
        on_device, mesh=mesh, in_specs=in_specs, out_specs=out_specs, check_vma=False
    )
```

```python
import functools

import jax
import jax.numpy as jnp
from jax import lax
from jax.experimental import pallas as pl
from jax.experimental.pallas import tpu as pltpu
from jax.sharding import PartitionSpec as P

MESH = pl.DeviceIdType.MESH
F32 = jnp.float32
BF16 = jnp.bfloat16

NX, NZ, NY = 4, 8, 4
TOK = 128
OWN = 16
ROWS = OWN * NX * NZ
SLOT = OWN * NX
CHUNKS = ((0,), (1, 2), (3, 4), (5, 6), (7,))
NCH = len(CHUNKS)
KEEPER = {0: 0, NCH - 1: 1}
EXT = 128
OFFSETS = (0, 1, -1, 2, -2, 3, -3, 4)

ORDER = (
    "GR:0", "GC:0", "A:0", "T:0", "B:0", "GR:1", "GC:1", "A:1",
    "D:0", "B:1", "E:0", "GR:2", "GC:2", "A:2", "F:0", "D:1",
    "B:2", "G:0", "GR:3", "GC:3", "A:3", "H:0", "E:1", "B:3",
    "A:4", "D:2", "F:1", "B:4", "G:1", "D:3", "E:2", "D:4",
    "H:1", "F:2", "E:4", "E:3", "G:2", "F:4", "F:3", "G:4",
    "G:3", "RX:0", "H:2", "WI:0", "WI:1", "WI:2", "H:4", "RZ:0",
    "WI:3", "WO:0", "WO:1", "WO:2", "WO:3", "H:3",
)


def encode(value, rows):
    wide = jnp.broadcast_to(value, (rows, EXT))
    high = wide.astype(BF16).astype(F32)
    lane = lax.broadcasted_iota(jnp.int32, (rows, EXT), 1)
    return jnp.where(lane < EXT // 2, high, wide - high).astype(BF16)


def decode(block):
    return block[:, 0:1].astype(F32) + block[:, EXT // 2 : EXT // 2 + 1].astype(F32)


def nt(a, b):
    return lax.dot_general(a, b, (((1,), (1,)), ((), ())), preferred_element_type=F32)


def tn(a, b):
    return lax.dot_general(a, b, (((0,), (0,)), ((), ())), preferred_element_type=F32)


def tiles(extent, step):
    return [(at, min(step, extent - at)) for at in range(0, extent, step)]


def kernel(
    D,
    F,
    hidden_hbm,
    rw_ref,
    teacher_ref,
    pos_ref,
    cot_ref,
    gw_hbm,
    uw_hbm,
    dw_hbm,
    hg_out,
    rg_ref,
    gg_out,
    ug_out,
    dg_out,
    hid,
    wgu,
    wd,
    agb,
    part,
    csend,
    crecv,
    ysend,
    yrecv,
    gact,
    rgf,
    xsend,
    xrecv,
    zown,
    zsend,
    zrecv,
    lsend,
    lrecv,
    rparts_x,
    rparts_z,
    tgrad,
    send_sem,
    recv_sem,
    local_sem,
):
    C = 3 * F + EXT
    H = C // 2
    wide, narrow = lax.axis_index("wide"), lax.axis_index("narrow")
    x, z = lax.div(wide, NZ), lax.rem(wide, NZ)
    y, core = lax.div(narrow, 2), lax.rem(narrow, 2)

    def at_x(d):
        return (lax.rem(x + d + NX, NX) * NZ + z, narrow)

    def at_z(d):
        return (x * NZ + lax.rem(z + d + NZ, NZ), narrow)

    def at_y(d):
        return (wide, lax.rem(y + d + NY, NY) * 2 + core)

    def at_n(d):
        return (wide, lax.rem(narrow + d, 2 * NY))

    sibling = (wide, y * 2 + (1 - core))

    count = [0]
    started = []

    def make(src, dst, device):
        i = count[0]
        count[0] += 1
        return pltpu.make_async_remote_copy(
            src_ref=src,
            dst_ref=dst,
            send_sem=send_sem.at[i],
            recv_sem=recv_sem.at[i],
            device_id=device,
            device_id_type=MESH,
        )

    def send(src, dst, device):
        copy = make(src, dst, device)
        copy.start()
        started.append(copy)
        return copy

    def on(core_of_chip, part):
        if core_of_chip is None:
            part()
        else:
            pl.when(core == core_of_chip)(part)

    lcount = [0]

    def local(src, dst):
        copy = pltpu.make_async_copy(src, dst, local_sem.at[lcount[0]])
        lcount[0] += 1
        copy.start()
        return copy

    load_hid = local(hidden_hbm, hid)
    load_w = [
        local(gw_hbm, wgu.at[:, pl.ds(0, F)]),
        local(uw_hbm, wgu.at[:, pl.ds(F, F)]),
        local(dw_hbm, wd),
    ]

    barrier = pltpu.get_barrier_semaphore()
    peers = (
        [at_x(d) for d in range(1, NX)]
        + [at_z(d) for d in range(1, NZ)]
        + [at_n(d) for d in range(1, 2 * NY)]
    )
    for peer in peers:
        pl.semaphore_signal(barrier, inc=1, device_id=peer, device_id_type=MESH)

    sub = lax.broadcasted_iota(jnp.int32, (OWN, TOK), 0)
    lane = lax.broadcasted_iota(jnp.int32, (OWN, TOK), 1)
    sub_t = lax.broadcasted_iota(jnp.int32, (TOK, OWN), 0)
    lane_t = lax.broadcasted_iota(jnp.int32, (TOK, OWN), 1)
    pick = jnp.zeros((OWN, TOK), F32)
    place = jnp.zeros((TOK, OWN), F32)
    half_own, half_tok = OWN // 2, TOK // 2
    for r in range(OWN):
        s, j = r // half_own, r % half_own
        token = pos_ref[s, wide * half_own + j] - wide * half_tok + s * half_tok
        pick = jnp.where((sub == r) & (lane == token), 1.0, pick)
        place = jnp.where((lane_t == r) & (sub_t == token), 1.0, place)
    load_hid.wait()
    own_rows = jnp.dot(pick.astype(BF16), hid[...], preferred_element_type=F32)
    agb[0, pl.ds(0, OWN), :] = own_rows.astype(BF16)
    agb[1, pl.ds(0, OWN), :] = jnp.concatenate(
        [cot_ref[0].astype(F32), cot_ref[1].astype(F32)], axis=0
    ).astype(BF16)
    pl.semaphore_wait(barrier, len(peers))

    def gather_x(which):
        own = agb.at[which, pl.ds(0, OWN)]
        return [
            send(own, agb.at[which, pl.ds((NX - d) * OWN, OWN)], at_x(d)) for d in (2, 1, 3)
        ]

    gx = {0: gather_x(0)}

    eye = lax.broadcasted_iota(jnp.int32, (TOK, TOK), 0) == lax.broadcasted_iota(
        jnp.int32, (TOK, TOK), 1
    )
    logit_col = jnp.sum(hid[...].astype(F32) * rw_ref[...], axis=1, keepdims=True)
    logit_row = jnp.sum(jnp.where(eye, logit_col, 0.0), axis=0, keepdims=True)
    lsend[...] = jnp.broadcast_to(logit_row, (8, TOK))
    gx[1] = gather_x(1)
    lg = [send(lsend, lrecv.at[d - 1], at_n(d)) for d in range(1, 2 * NY)]

    gz = {}

    def ring(which, src, dst, d, at=0, n=SLOT):
        return send(
            agb.at[which, pl.ds(src * SLOT + at, n)],
            agb.at[which, pl.ds(dst * SLOT + at, n)],
            at_z(d),
        )

    def gather(which, step):
        for copy in gx[which] if step == 0 else gz[which, step]:
            copy.wait_recv()
        if step == 0:
            gz[which, 1] = [ring(which, 0, 1, -1), ring(which, 0, 2, 1)]
        elif step == 1:
            gz[which, 2] = [ring(which, 1, 3, -1), ring(which, 2, 4, 1)]
        elif step == 2:
            gz[which, 3] = [ring(which, 3, 5, -1), ring(which, 4, 6, 1)]
        elif step == 3:
            half = SLOT // 2
            gz[which, 4] = [
                ring(which, 5, 7, -1, 0, half),
                ring(which, 6, 7, 1, half, half),
            ]

    core_out, y_out, g_first, g_second, core_back, x_out, z_out = ({} for _ in range(7))

    def block(j, base=0):
        return pl.ds(pl.multiple_of(base + lax.rem(y + j + NY, NY) * OWN, OWN), OWN)

    def chunk(i):
        base, rows = CHUNKS[i][0] * SLOT, len(CHUNKS[i]) * SLOT
        keeper = KEEPER.get(i)
        share = base if keeper is not None else base + core * SLOT
        return keeper, base, rows, share

    def stage1(i):
        keeper, base, n, _ = chunk(i)
        rows = pl.ds(base, n)
        if i == 0:
            for copy in load_w:
                copy.wait()
        if i == NCH - 1:
            for which in (0, 1):
                for copy in gz[which, 4]:
                    copy.wait_recv()
        for at, m in tiles(2 * F, 256):
            cols = pl.ds(at, m)
            part[rows, cols] = jnp.dot(
                agb[0, rows, :], wgu[:, cols], preferred_element_type=F32
            )
        for at, m in tiles(F, 256):
            part[rows, pl.ds(2 * F + at, m)] = nt(agb[1, rows, :], wd[pl.ds(at, m), :])
        logit = jnp.sum(agb[0, rows, :].astype(F32) * rw_ref[...], axis=1, keepdims=True)
        part[rows, pl.ds(3 * F, EXT)] = jnp.broadcast_to(logit, (n, EXT))
        if keeper is None:
            other = pl.ds(pl.multiple_of(base + (1 - core) * SLOT, SLOT), SLOT)
        else:
            other = rows
        copy = make(csend.at[i], crecv.at[i], sibling)
        core_out[i] = copy

        def to_other():
            csend[i, :, pl.ds(0, 3 * F)] = part[other, pl.ds(0, 3 * F)].astype(BF16)
            csend[i, :, pl.ds(3 * F, EXT)] = encode(
                part[other, pl.ds(3 * F, EXT)][:, 0:1], SLOT
            )
            copy.start()

        on(None if keeper is None else 1 - keeper, to_other)

    def stage2(i):
        keeper, _, _, share = chunk(i)
        mine = pl.ds(share if keeper is not None else pl.multiple_of(share, SLOT), SLOT)
        copies = [
            make(ysend.at[i, block(d)], yrecv.at[i, d - 1], at_y(d)) for d in (2, 1, 3)
        ]
        y_out[i] = copies

        def add():
            core_out[i].wait_recv()
            total = part[mine, pl.ds(0, 3 * F)] + crecv[i, :, pl.ds(0, 3 * F)].astype(F32)
            part[mine, pl.ds(0, 3 * F)] = total
            ysend[i, :, pl.ds(0, 3 * F)] = total.astype(BF16)
            logit = part[mine, pl.ds(3 * F, EXT)][:, 0:1] + decode(
                crecv[i, :, pl.ds(3 * F, EXT)]
            )
            part[mine, pl.ds(3 * F, EXT)] = jnp.broadcast_to(logit, (SLOT, EXT))
            ysend[i, :, pl.ds(3 * F, EXT)] = encode(logit, SLOT)
            for copy in copies:
                copy.start()

        on(keeper, add)

    def stage4(i):
        keeper, _, _, share = chunk(i)
        own = block(0, share)
        ext = pl.ds(3 * F, EXT)
        copies = [make(gact.at[own], gact.at[own], at_y(d)) for d in (1, -1)]
        g_first[i] = copies

        def gate_block():
            for copy in y_out[i]:
                copy.wait_recv()

            def total(at):
                cols = pl.ds(at, F)
                value = part[own, cols]
                for d in range(NY - 1):
                    value = value + yrecv[i, d, :, cols].astype(F32)
                return value

            logit = part[own, ext][:, 0:1]
            for d in range(NY - 1):
                logit = logit + decode(yrecv[i, d, :, ext])
            scale = jax.nn.sigmoid(logit)
            gate, up, raw = total(0), total(F), total(2 * F)
            sig = jax.nn.sigmoid(gate)
            silu = gate * sig
            act = silu * up
            act_grad = scale * raw
            gate_pre = act_grad * up * sig * (1.0 + gate * (1.0 - sig))
            gact[own, pl.ds(0, F)] = gate_pre.astype(BF16)
            gact[own, pl.ds(F, F)] = (act_grad * silu).astype(BF16)
            gact[own, pl.ds(2 * F, F)] = (scale * act).astype(BF16)
            dots = jnp.sum(act * raw, axis=1, keepdims=True)
            gact[own, ext] = encode(scale * (1.0 - scale) * dots, OWN)
            for copy in copies:
                copy.start()

        on(keeper, gate_block)

    def stage5(i):
        keeper, _, _, share = chunk(i)
        left = gact.at[block(-1, share), pl.ds(0, H)]
        right = gact.at[block(1, share), pl.ds(H, H)]
        copies = [make(left, left, at_y(1)), make(right, right, at_y(-1))]
        g_second[i] = copies

        def hand_on():
            for first, second in zip(g_first[i], copies):
                first.wait_recv()
                second.start()

        on(keeper, hand_on)

    def stage6(i):
        keeper, _, _, share = chunk(i)
        start = share if keeper is not None else pl.multiple_of(share, SLOT)
        half = gact.at[pl.ds(start, SLOT)]
        copy = make(half, half, sibling)
        core_back[i] = copy

        def give():
            for second in g_second[i]:
                second.wait_recv()
            copy.start()

        on(keeper, give)

    def stage7(i):
        keeper, base, n, _ = chunk(i)
        on(None if keeper is None else 1 - keeper, core_back[i].wait_recv)
        rows = pl.ds(base, n)
        routed = decode(gact[rows, pl.ds(3 * F, EXT)])
        for at, m in tiles(D, 256):
            cols = pl.ds(at, m)
            out = nt(gact[rows, pl.ds(0, 2 * F)], wgu[cols, :]) + routed * rw_ref[:, cols]
            for s, k in enumerate(CHUNKS[i]):
                for j in range(NX):
                    piece = out[s * SLOT + j * OWN : s * SLOT + (j + 1) * OWN]
                    if j == 0:
                        rgf[k, :, cols] = piece
                    else:
                        xsend[k, j - 1, :, cols] = piece.astype(BF16)
        slots = pl.ds(CHUNKS[i][0], len(CHUNKS[i]))
        x_out[i] = [
            send(xsend.at[slots, j - 1], xrecv.at[slots, j - 1], at_x(j)) for j in (2, 1, 3)
        ]

    def stage8(i):
        for copy in x_out[i]:
            copy.wait_recv()
        for k in CHUNKS[i]:
            total = rgf[k]
            for j in range(NX - 1):
                total = total + xrecv[k, j].astype(F32)
            if k == 0:
                zown[...] = total
            else:
                zsend[k - 1] = total.astype(BF16)
                z_out[k] = send(zsend.at[k - 1], zrecv.at[k - 1], at_z(OFFSETS[k]))

    held = {}

    def own_tokens():
        for copy in lg:
            copy.wait_recv()
        logits = lsend[0:1, :]
        for d in range(2 * NY - 1):
            logits = logits + lrecv[d, 0:1, :]
        logit_col = jnp.sum(jnp.where(eye, logits, 0.0), axis=1, keepdims=True)
        eye_half = lax.broadcasted_iota(jnp.int32, (half_tok, half_tok), 0) == (
            lax.broadcasted_iota(jnp.int32, (half_tok, half_tok), 1)
        )
        teacher = jnp.concatenate(
            [
                jnp.sum(jnp.where(eye_half, teacher_ref[s : s + 1, :], 0.0), axis=1, keepdims=True)
                for s in range(2)
            ],
            axis=0,
        )
        grad = jax.nn.sigmoid(logit_col) - teacher
        router = jnp.sum(grad * hid[...].astype(F32), axis=0, keepdims=True)
        for a in range(D // 128):
            rparts_x[x, a : a + 1, :] = router[:, a * 128 : (a + 1) * 128]
        tgrad[...] = jnp.broadcast_to(grad, (TOK, 128))

    def router_x():
        routed = tn(gact[:, pl.ds(3 * F, EXT)], agb[0])
        routed = routed[0:1] + routed[EXT // 2 : EXT // 2 + 1]
        for a in range(D // 128):
            rparts_x[x, a : a + 1, :] += routed[:, a * 128 : (a + 1) * 128]
        held["rx"] = [send(rparts_x.at[x], rparts_x.at[x], at_x(d)) for d in range(1, NX)]

    def router_z():
        for copy in held["rx"]:
            copy.wait_recv()
        rparts_z[z] = rparts_x[0] + rparts_x[1] + rparts_x[2] + rparts_x[3]
        held["rz"] = [send(rparts_z.at[z], rparts_z.at[z], at_z(d)) for d in range(1, NZ)]

    def grads_in(t):
        cols = pl.ds(t * 256, 256)
        out = tn(agb[0, :, cols], gact[:, pl.ds(0, 2 * F)])
        gg_out[cols, :] = out[:, :F].astype(BF16)
        ug_out[cols, :] = out[:, F:].astype(BF16)

    def grads_out(t):
        at, n = tiles(F, 256)[t]
        dg_out[pl.ds(at, n), :] = tn(gact[:, pl.ds(2 * F + at, n)], agb[1]).astype(BF16)

    tasks = {
        "GR": lambda step: gather(0, step),
        "GC": lambda step: gather(1, step),
        "A": stage1,
        "B": stage2,
        "D": stage4,
        "E": stage5,
        "F": stage6,
        "G": stage7,
        "H": stage8,
        "T": lambda _: own_tokens(),
        "RX": lambda _: router_x(),
        "RZ": lambda _: router_z(),
        "WI": grads_in,
        "WO": grads_out,
    }
    for task in ORDER:
        name, step = task.split(":")
        tasks[name](int(step))

    late = list(z_out.values()) + held["rz"]
    late_ids = [id(copy) for copy in late]
    for copy in started:
        if id(copy) not in late_ids:
            copy.wait_send()
    for i in range(NCH):
        keeper = KEEPER.get(i)

        def sent(keeper=keeper, i=i):
            for copy in y_out[i] + g_first[i] + g_second[i] + [core_back[i]]:
                copy.wait_send()

        on(keeper, sent)
        on(None if keeper is None else 1 - keeper, core_out[i].wait_send)

    for k in range(1, NZ):
        z_out[k].wait_recv()
    total = zown[...]
    for k in range(NZ - 1):
        total = total + zrecv[k].astype(F32)
    high = total.astype(BF16)
    low = (total - high.astype(F32)).astype(BF16)
    place16 = place.astype(BF16)
    hg_out[...] = (
        tgrad[:, 0:1] * rw_ref[...]
        + jnp.dot(place16, high, preferred_element_type=F32)
        + jnp.dot(place16, low, preferred_element_type=F32)
    ).astype(BF16)

    for copy in held["rz"]:
        copy.wait_recv()
    final = rparts_z[0]
    for k in range(1, NZ):
        final = final + rparts_z[k]
    for a in range(D // 128):
        rg_ref[:, a * 128 : (a + 1) * 128] = final[a : a + 1, :]

    for copy in late:
        copy.wait_send()


def store_kernel(*refs):
    n = len(refs) // 2
    sems = refs[-1]
    copies = [pltpu.make_async_copy(refs[i], refs[n + i], sems.at[i]) for i in range(n)]
    for copy in copies:
        copy.start()
    for copy in copies:
        copy.wait()


def store(arrays):
    arrays = [pltpu.with_memory_space_constraint(a, pltpu.VMEM) for a in arrays]
    return pl.pallas_call(
        store_kernel,
        out_shape=tuple(jax.ShapeDtypeStruct(a.shape, a.dtype) for a in arrays),
        in_specs=[pl.BlockSpec(memory_space=pltpu.VMEM)] * len(arrays),
        out_specs=(pl.BlockSpec(memory_space=pl.ANY),) * len(arrays),
        scratch_shapes=[pltpu.SemaphoreType.DMA((len(arrays),))],
        compiler_params=pltpu.CompilerParams(vmem_limit_bytes=8 * 1024 * 1024),
    )(*arrays)


def on_device(
    hidden, router_weight, teacher, positions, cotangent, gate_weight, up_weight, down_weight
):
    slabs, rows_dev, D = hidden.shape
    F = gate_weight.shape[1]
    C = 3 * F + EXT
    vmem = pl.BlockSpec(memory_space=pltpu.VMEM)
    smem = pl.BlockSpec(memory_space=pltpu.SMEM)
    hbm = pl.BlockSpec(memory_space=pl.ANY)
    copies = 6 + 16 + 7 + NCH * 12 + 7 + 3 + 7
    hidden_grad, router_grad, gate_grad, up_grad, down_grad = pl.pallas_call(
        functools.partial(kernel, D, F),
        out_shape=(
            pltpu.VMEM((TOK, D), BF16),
            pltpu.VMEM((1, D), F32),
            pltpu.VMEM((D, F), BF16),
            pltpu.VMEM((D, F), BF16),
            pltpu.VMEM((F, D), BF16),
        ),
        in_specs=[hbm, vmem, vmem, smem, vmem, hbm, hbm, hbm],
        out_specs=(vmem,)*5,
        scratch_shapes=[
            pltpu.VMEM((TOK, D), BF16),
            pltpu.VMEM((D, 2 * F), BF16),
            pltpu.VMEM((F, D), BF16),
            pltpu.VMEM((2, ROWS, D), BF16),
            pltpu.VMEM((ROWS, C), F32),
            pltpu.VMEM((NCH, SLOT, C), BF16),
            pltpu.VMEM((NCH, SLOT, C), BF16),
            pltpu.VMEM((NCH, SLOT, C), BF16),
            pltpu.VMEM((NCH, NY - 1, OWN, C), BF16),
            pltpu.VMEM((ROWS, C), BF16),
            pltpu.VMEM((NZ, OWN, D), F32),
            pltpu.VMEM((NZ, NX - 1, OWN, D), BF16),
            pltpu.VMEM((NZ, NX - 1, OWN, D), BF16),
            pltpu.VMEM((OWN, D), F32),
            pltpu.VMEM((NZ - 1, OWN, D), BF16),
            pltpu.VMEM((NZ - 1, OWN, D), BF16),
            pltpu.VMEM((8, TOK), F32),
            pltpu.VMEM((2 * NY - 1, 8, TOK), F32),
            pltpu.VMEM((NX, D // 128, 128), F32),
            pltpu.VMEM((NZ, D // 128, 128), F32),
            pltpu.VMEM((TOK, 128), F32),
            pltpu.SemaphoreType.DMA((copies,)),
            pltpu.SemaphoreType.DMA((copies,)),
            pltpu.SemaphoreType.DMA((8,)),
        ],
        compiler_params=pltpu.CompilerParams(
            collective_id=0,
            has_side_effects=True,
            vmem_limit_bytes=58 * 1024 * 1024,
        ),
    )(
        hidden.reshape(slabs * rows_dev, D),
        router_weight.reshape(1, D),
        teacher,
        positions,
        cotangent,
        gate_weight,
        up_weight,
        down_weight,
    )
    hidden_grad, router_grad, gate_grad, up_grad, down_grad = store(
        (hidden_grad, router_grad, gate_grad, up_grad, down_grad)
    )
    return (
        hidden_grad.reshape(hidden.shape),
        router_grad.reshape(D),
        gate_grad,
        up_grad,
        down_grad,
    )


def solution(mesh):
    in_specs = (
        P(None, "wide", "narrow"),
        P("narrow"),
        P(None, "wide"),
        P(),
        P(None, "wide", "narrow"),
        P("narrow", "wide"),
        P("narrow", "wide"),
        P("wide", "narrow"),
    )
    out_specs = (
        P(None, "wide", "narrow"),
        P("narrow"),
        P("narrow", "wide"),
        P("narrow", "wide"),
        P("wide", "narrow"),
    )
    return jax.shard_map(
        on_device, mesh=mesh, in_specs=in_specs, out_specs=out_specs, check_vma=False
    )
```

```python
import functools

import jax
import jax.numpy as jnp
from jax import lax
from jax.experimental import pallas as pl
from jax.experimental.pallas import tpu as pltpu
from jax.sharding import PartitionSpec as P

MESH = pl.DeviceIdType.MESH
F32 = jnp.float32
BF16 = jnp.bfloat16

NX, NZ, NY = 4, 8, 4
TOK = 128
OWN = 16
ROWS = OWN * NX * NZ
SLOT = OWN * NX
CHUNKS = ((0,), (1, 2), (3, 4), (5, 6), (7,))
NCH = len(CHUNKS)
KEEPER = {0: 0, NCH - 1: 1}
EXT = 128
OFFSETS = (0, 1, -1, 2, -2, 3, -3, 4)

ORDER = (
    "GR:0", "GC:0", "A:0", "T:0", "B:0", "GR:1", "GC:1", "A:1",
    "D:0", "GR:2", "B:1", "E:0", "GC:2", "A:2", "GR:3", "B:2",
    "D:1", "F:0", "GC:3", "A:3", "G:0", "B:3", "A:4", "D:2",
    "H:0", "E:1", "B:4", "D:3", "E:2", "F:1", "D:4", "G:1",
    "E:3", "F:2", "E:4", "G:2", "F:3", "F:4", "H:1", "G:3",
    "G:4", "RX:0", "WI:0", "H:2", "WI:1", "WI:2", "WI:3", "WO:0",
    "WO:1", "H:3", "WO:2", "WO:3", "H:4", "RZ:0",
)


def encode(value, rows):
    wide = jnp.broadcast_to(value, (rows, EXT))
    high = wide.astype(BF16).astype(F32)
    lane = lax.broadcasted_iota(jnp.int32, (rows, EXT), 1)
    return jnp.where(lane < EXT // 2, high, wide - high).astype(BF16)


def decode(block):
    return block[:, 0:1].astype(F32) + block[:, EXT // 2 : EXT // 2 + 1].astype(F32)


def nt(a, b):
    return lax.dot_general(a, b, (((1,), (1,)), ((), ())), preferred_element_type=F32)


def tn(a, b):
    return lax.dot_general(a, b, (((0,), (0,)), ((), ())), preferred_element_type=F32)


def tiles(extent, step):
    return [(at, min(step, extent - at)) for at in range(0, extent, step)]


def kernel(
    D,
    F,
    hidden_hbm,
    rw_ref,
    teacher_ref,
    pos_ref,
    cot_ref,
    gw_hbm,
    uw_hbm,
    dw_hbm,
    hg_out,
    rg_ref,
    gg_out,
    ug_out,
    dg_out,
    hid,
    wgu,
    wd,
    agb,
    part,
    csend,
    crecv,
    ysend,
    yrecv,
    gact,
    rgf,
    xsend,
    xrecv,
    zown,
    zsend,
    zrecv,
    lsend,
    lrecv,
    rparts_x,
    rparts_z,
    tgrad,
    send_sem,
    recv_sem,
    local_sem,
):
    C = 3 * F + EXT
    H = C // 2
    wide, narrow = lax.axis_index("wide"), lax.axis_index("narrow")
    x, z = lax.div(wide, NZ), lax.rem(wide, NZ)
    y, core = lax.div(narrow, 2), lax.rem(narrow, 2)

    def at_x(d):
        return (lax.rem(x + d + NX, NX) * NZ + z, narrow)

    def at_z(d):
        return (x * NZ + lax.rem(z + d + NZ, NZ), narrow)

    def at_y(d):
        return (wide, lax.rem(y + d + NY, NY) * 2 + core)

    def at_n(d):
        return (wide, lax.rem(narrow + d, 2 * NY))

    sibling = (wide, y * 2 + (1 - core))

    count = [0]
    started = []

    def make(src, dst, device):
        i = count[0]
        count[0] += 1
        return pltpu.make_async_remote_copy(
            src_ref=src,
            dst_ref=dst,
            send_sem=send_sem.at[i],
            recv_sem=recv_sem.at[i],
            device_id=device,
            device_id_type=MESH,
        )

    def send(src, dst, device):
        copy = make(src, dst, device)
        copy.start()
        started.append(copy)
        return copy

    def on(core_of_chip, part):
        if core_of_chip is None:
            part()
        else:
            pl.when(core == core_of_chip)(part)

    lcount = [0]

    def local(src, dst):
        copy = pltpu.make_async_copy(src, dst, local_sem.at[lcount[0]])
        lcount[0] += 1
        copy.start()
        return copy

    load_hid = local(hidden_hbm, hid)
    load_w = [
        local(gw_hbm, wgu.at[:, pl.ds(0, F)]),
        local(uw_hbm, wgu.at[:, pl.ds(F, F)]),
        local(dw_hbm, wd),
    ]

    barrier = pltpu.get_barrier_semaphore()
    peers = (
        [at_x(d) for d in range(1, NX)]
        + [at_z(d) for d in range(1, NZ)]
        + [at_n(d) for d in range(1, 2 * NY)]
    )
    for peer in peers:
        pl.semaphore_signal(barrier, inc=1, device_id=peer, device_id_type=MESH)

    sub = lax.broadcasted_iota(jnp.int32, (OWN, TOK), 0)
    lane = lax.broadcasted_iota(jnp.int32, (OWN, TOK), 1)
    sub_t = lax.broadcasted_iota(jnp.int32, (TOK, OWN), 0)
    lane_t = lax.broadcasted_iota(jnp.int32, (TOK, OWN), 1)
    pick = jnp.zeros((OWN, TOK), F32)
    place = jnp.zeros((TOK, OWN), F32)
    half_own, half_tok = OWN // 2, TOK // 2
    for r in range(OWN):
        s, j = r // half_own, r % half_own
        token = pos_ref[s, wide * half_own + j] - wide * half_tok + s * half_tok
        pick = jnp.where((sub == r) & (lane == token), 1.0, pick)
        place = jnp.where((lane_t == r) & (sub_t == token), 1.0, place)
    load_hid.wait()
    own_rows = jnp.dot(pick.astype(BF16), hid[...], preferred_element_type=F32)
    agb[0, pl.ds(0, OWN), :] = own_rows.astype(BF16)
    agb[1, pl.ds(0, OWN), :] = jnp.concatenate(
        [cot_ref[0].astype(F32), cot_ref[1].astype(F32)], axis=0
    ).astype(BF16)
    pl.semaphore_wait(barrier, len(peers))

    def gather_x(which):
        own = agb.at[which, pl.ds(0, OWN)]
        return [
            send(own, agb.at[which, pl.ds((NX - d) * OWN, OWN)], at_x(d)) for d in (2, 1, 3)
        ]

    gx = {0: gather_x(0)}

    eye = lax.broadcasted_iota(jnp.int32, (TOK, TOK), 0) == lax.broadcasted_iota(
        jnp.int32, (TOK, TOK), 1
    )
    logit_col = jnp.sum(hid[...].astype(F32) * rw_ref[...], axis=1, keepdims=True)
    logit_row = jnp.sum(jnp.where(eye, logit_col, 0.0), axis=0, keepdims=True)
    lsend[...] = jnp.broadcast_to(logit_row, (8, TOK))
    gx[1] = gather_x(1)
    lg = [send(lsend, lrecv.at[d - 1], at_n(d)) for d in range(1, 2 * NY)]

    gz = {}

    def ring(which, src, dst, d, at=0, n=SLOT):
        return send(
            agb.at[which, pl.ds(src * SLOT + at, n)],
            agb.at[which, pl.ds(dst * SLOT + at, n)],
            at_z(d),
        )

    def gather(which, step):
        for copy in gx[which] if step == 0 else gz[which, step]:
            copy.wait_recv()
        if step == 0:
            gz[which, 1] = [ring(which, 0, 1, -1), ring(which, 0, 2, 1)]
        elif step == 1:
            gz[which, 2] = [ring(which, 1, 3, -1), ring(which, 2, 4, 1)]
        elif step == 2:
            gz[which, 3] = [ring(which, 3, 5, -1), ring(which, 4, 6, 1)]
        elif step == 3:
            half = SLOT // 2
            gz[which, 4] = [
                ring(which, 5, 7, -1, 0, half),
                ring(which, 6, 7, 1, half, half),
            ]

    core_out, y_out, g_first, g_second, core_back, x_out, z_out = ({} for _ in range(7))

    def block(j, base=0):
        return pl.ds(pl.multiple_of(base + lax.rem(y + j + NY, NY) * OWN, OWN), OWN)

    def chunk(i):
        base, rows = CHUNKS[i][0] * SLOT, len(CHUNKS[i]) * SLOT
        keeper = KEEPER.get(i)
        share = base if keeper is not None else base + core * SLOT
        return keeper, base, rows, share

    def stage1(i):
        keeper, base, n, _ = chunk(i)
        rows = pl.ds(base, n)
        if i == 0:
            for copy in load_w:
                copy.wait()
        if i == NCH - 1:
            for which in (0, 1):
                for copy in gz[which, 4]:
                    copy.wait_recv()
        for at, m in tiles(2 * F, 256):
            cols = pl.ds(at, m)
            part[rows, cols] = jnp.dot(
                agb[0, rows, :], wgu[:, cols], preferred_element_type=F32
            )
        for at, m in tiles(F, 256):
            part[rows, pl.ds(2 * F + at, m)] = nt(agb[1, rows, :], wd[pl.ds(at, m), :])
        logit = jnp.sum(agb[0, rows, :].astype(F32) * rw_ref[...], axis=1, keepdims=True)
        part[rows, pl.ds(3 * F, EXT)] = jnp.broadcast_to(logit, (n, EXT))
        if keeper is None:
            other = pl.ds(pl.multiple_of(base + (1 - core) * SLOT, SLOT), SLOT)
        else:
            other = rows
        copy = make(csend.at[i], crecv.at[i], sibling)
        core_out[i] = copy

        def to_other():
            csend[i, :, pl.ds(0, 3 * F)] = part[other, pl.ds(0, 3 * F)].astype(BF16)
            csend[i, :, pl.ds(3 * F, EXT)] = encode(
                part[other, pl.ds(3 * F, EXT)][:, 0:1], SLOT
            )
            copy.start()

        on(None if keeper is None else 1 - keeper, to_other)

    def stage2(i):
        keeper, _, _, share = chunk(i)
        mine = pl.ds(share if keeper is not None else pl.multiple_of(share, SLOT), SLOT)
        copies = [
            make(ysend.at[i, block(d)], yrecv.at[i, d - 1], at_y(d)) for d in (2, 1, 3)
        ]
        y_out[i] = copies

        def add():
            core_out[i].wait_recv()
            total = part[mine, pl.ds(0, 3 * F)] + crecv[i, :, pl.ds(0, 3 * F)].astype(F32)
            part[mine, pl.ds(0, 3 * F)] = total
            ysend[i, :, pl.ds(0, 3 * F)] = total.astype(BF16)
            logit = part[mine, pl.ds(3 * F, EXT)][:, 0:1] + decode(
                crecv[i, :, pl.ds(3 * F, EXT)]
            )
            part[mine, pl.ds(3 * F, EXT)] = jnp.broadcast_to(logit, (SLOT, EXT))
            ysend[i, :, pl.ds(3 * F, EXT)] = encode(logit, SLOT)
            for copy in copies:
                copy.start()

        on(keeper, add)

    def stage4(i):
        keeper, _, _, share = chunk(i)
        own = block(0, share)
        ext = pl.ds(3 * F, EXT)
        copies = [make(gact.at[own], gact.at[own], at_y(d)) for d in (1, -1)]
        g_first[i] = copies

        def gate_block():
            for copy in y_out[i]:
                copy.wait_recv()

            def total(at):
                cols = pl.ds(at, F)
                value = part[own, cols]
                for d in range(NY - 1):
                    value = value + yrecv[i, d, :, cols].astype(F32)
                return value

            logit = part[own, ext][:, 0:1]
            for d in range(NY - 1):
                logit = logit + decode(yrecv[i, d, :, ext])
            scale = jax.nn.sigmoid(logit)
            gate, up, raw = total(0), total(F), total(2 * F)
            sig = jax.nn.sigmoid(gate)
            silu = gate * sig
            act = silu * up
            act_grad = scale * raw
            gate_pre = act_grad * up * sig * (1.0 + gate * (1.0 - sig))
            gact[own, pl.ds(0, F)] = gate_pre.astype(BF16)
            gact[own, pl.ds(F, F)] = (act_grad * silu).astype(BF16)
            gact[own, pl.ds(2 * F, F)] = (scale * act).astype(BF16)
            dots = jnp.sum(act * raw, axis=1, keepdims=True)
            gact[own, ext] = encode(scale * (1.0 - scale) * dots, OWN)
            for copy in copies:
                copy.start()

        on(keeper, gate_block)

    def stage5(i):
        keeper, _, _, share = chunk(i)
        left = gact.at[block(-1, share), pl.ds(0, H)]
        right = gact.at[block(1, share), pl.ds(H, H)]
        copies = [make(left, left, at_y(1)), make(right, right, at_y(-1))]
        g_second[i] = copies

        def hand_on():
            for first, second in zip(g_first[i], copies):
                first.wait_recv()
                second.start()

        on(keeper, hand_on)

    def stage6(i):
        keeper, _, _, share = chunk(i)
        start = share if keeper is not None else pl.multiple_of(share, SLOT)
        half = gact.at[pl.ds(start, SLOT)]
        copy = make(half, half, sibling)
        core_back[i] = copy

        def give():
            for second in g_second[i]:
                second.wait_recv()
            copy.start()

        on(keeper, give)

    def stage7(i):
        keeper, base, n, _ = chunk(i)
        on(None if keeper is None else 1 - keeper, core_back[i].wait_recv)
        rows = pl.ds(base, n)
        routed = decode(gact[rows, pl.ds(3 * F, EXT)])
        for at, m in tiles(D, 256):
            cols = pl.ds(at, m)
            out = nt(gact[rows, pl.ds(0, 2 * F)], wgu[cols, :]) + routed * rw_ref[:, cols]
            for s, k in enumerate(CHUNKS[i]):
                for j in range(NX):
                    piece = out[s * SLOT + j * OWN : s * SLOT + (j + 1) * OWN]
                    if j == 0:
                        rgf[k, :, cols] = piece
                    else:
                        xsend[k, j - 1, :, cols] = piece.astype(BF16)
        slots = pl.ds(CHUNKS[i][0], len(CHUNKS[i]))
        x_out[i] = [
            send(xsend.at[slots, j - 1], xrecv.at[slots, j - 1], at_x(j)) for j in (2, 1, 3)
        ]

    def stage8(i):
        for copy in x_out[i]:
            copy.wait_recv()
        for k in CHUNKS[i]:
            total = rgf[k]
            for j in range(NX - 1):
                total = total + xrecv[k, j].astype(F32)
            if k == 0:
                zown[...] = total
            else:
                zsend[k - 1] = total.astype(BF16)
                z_out[k] = send(zsend.at[k - 1], zrecv.at[k - 1], at_z(OFFSETS[k]))

    held = {}

    def own_tokens():
        for copy in lg:
            copy.wait_recv()
        logits = lsend[0:1, :]
        for d in range(2 * NY - 1):
            logits = logits + lrecv[d, 0:1, :]
        logit_col = jnp.sum(jnp.where(eye, logits, 0.0), axis=1, keepdims=True)
        eye_half = lax.broadcasted_iota(jnp.int32, (half_tok, half_tok), 0) == (
            lax.broadcasted_iota(jnp.int32, (half_tok, half_tok), 1)
        )
        teacher = jnp.concatenate(
            [
                jnp.sum(jnp.where(eye_half, teacher_ref[s : s + 1, :], 0.0), axis=1, keepdims=True)
                for s in range(2)
            ],
            axis=0,
        )
        grad = jax.nn.sigmoid(logit_col) - teacher
        router = jnp.sum(grad * hid[...].astype(F32), axis=0, keepdims=True)
        for a in range(D // 128):
            rparts_x[x, a : a + 1, :] = router[:, a * 128 : (a + 1) * 128]
        tgrad[...] = jnp.broadcast_to(grad, (TOK, 128))

    def router_x():
        routed = tn(gact[:, pl.ds(3 * F, EXT)], agb[0])
        routed = routed[0:1] + routed[EXT // 2 : EXT // 2 + 1]
        for a in range(D // 128):
            rparts_x[x, a : a + 1, :] += routed[:, a * 128 : (a + 1) * 128]
        held["rx"] = [send(rparts_x.at[x], rparts_x.at[x], at_x(d)) for d in range(1, NX)]

    def router_z():
        for copy in held["rx"]:
            copy.wait_recv()
        rparts_z[z] = rparts_x[0] + rparts_x[1] + rparts_x[2] + rparts_x[3]
        held["rz"] = [send(rparts_z.at[z], rparts_z.at[z], at_z(d)) for d in range(1, NZ)]

    def grads_in(t):
        cols = pl.ds(t * 256, 256)
        out = tn(agb[0, :, cols], gact[:, pl.ds(0, 2 * F)])
        gg_out[cols, :] = out[:, :F].astype(BF16)
        ug_out[cols, :] = out[:, F:].astype(BF16)

    def grads_out(t):
        at, n = tiles(F, 256)[t]
        dg_out[pl.ds(at, n), :] = tn(gact[:, pl.ds(2 * F + at, n)], agb[1]).astype(BF16)

    tasks = {
        "GR": lambda step: gather(0, step),
        "GC": lambda step: gather(1, step),
        "A": stage1,
        "B": stage2,
        "D": stage4,
        "E": stage5,
        "F": stage6,
        "G": stage7,
        "H": stage8,
        "T": lambda _: own_tokens(),
        "RX": lambda _: router_x(),
        "RZ": lambda _: router_z(),
        "WI": grads_in,
        "WO": grads_out,
    }
    for task in ORDER:
        name, step = task.split(":")
        tasks[name](int(step))

    late = list(z_out.values()) + held["rz"]
    late_ids = [id(copy) for copy in late]
    for copy in started:
        if id(copy) not in late_ids:
            copy.wait_send()
    for i in range(NCH):
        keeper = KEEPER.get(i)

        def sent(keeper=keeper, i=i):
            for copy in y_out[i] + g_first[i] + g_second[i] + [core_back[i]]:
                copy.wait_send()

        on(keeper, sent)
        on(None if keeper is None else 1 - keeper, core_out[i].wait_send)

    for k in range(1, NZ):
        z_out[k].wait_recv()
    total = zown[...]
    for k in range(NZ - 1):
        total = total + zrecv[k].astype(F32)
    high = total.astype(BF16)
    low = (total - high.astype(F32)).astype(BF16)
    place16 = place.astype(BF16)
    hg_out[...] = (
        tgrad[:, 0:1] * rw_ref[...]
        + jnp.dot(place16, high, preferred_element_type=F32)
        + jnp.dot(place16, low, preferred_element_type=F32)
    ).astype(BF16)

    for copy in held["rz"]:
        copy.wait_recv()
    final = rparts_z[0]
    for k in range(1, NZ):
        final = final + rparts_z[k]
    for a in range(D // 128):
        rg_ref[:, a * 128 : (a + 1) * 128] = final[a : a + 1, :]

    for copy in late:
        copy.wait_send()


def store_kernel(*refs):
    n = len(refs) // 2
    sems = refs[-1]
    copies = [pltpu.make_async_copy(refs[i], refs[n + i], sems.at[i]) for i in range(n)]
    for copy in copies:
        copy.start()
    for copy in copies:
        copy.wait()


def store(arrays):
    arrays = [pltpu.with_memory_space_constraint(a, pltpu.VMEM) for a in arrays]
    return pl.pallas_call(
        store_kernel,
        out_shape=tuple(jax.ShapeDtypeStruct(a.shape, a.dtype) for a in arrays),
        in_specs=[pl.BlockSpec(memory_space=pltpu.VMEM)] * len(arrays),
        out_specs=(pl.BlockSpec(memory_space=pl.ANY),) * len(arrays),
        scratch_shapes=[pltpu.SemaphoreType.DMA((len(arrays),))],
        compiler_params=pltpu.CompilerParams(vmem_limit_bytes=8 * 1024 * 1024),
    )(*arrays)


def on_device(
    hidden, router_weight, teacher, positions, cotangent, gate_weight, up_weight, down_weight
):
    slabs, rows_dev, D = hidden.shape
    F = gate_weight.shape[1]
    C = 3 * F + EXT
    vmem = pl.BlockSpec(memory_space=pltpu.VMEM)
    smem = pl.BlockSpec(memory_space=pltpu.SMEM)
    hbm = pl.BlockSpec(memory_space=pl.ANY)
    copies = 6 + 16 + 7 + NCH * 12 + 7 + 3 + 7
    hidden_grad, router_grad, gate_grad, up_grad, down_grad = pl.pallas_call(
        functools.partial(kernel, D, F),
        out_shape=(
            pltpu.VMEM((TOK, D), BF16),
            pltpu.VMEM((1, D), F32),
            pltpu.VMEM((D, F), BF16),
            pltpu.VMEM((D, F), BF16),
            pltpu.VMEM((F, D), BF16),
        ),
        in_specs=[hbm, vmem, vmem, smem, vmem, hbm, hbm, hbm],
        out_specs=(vmem,)*5,
        scratch_shapes=[
            pltpu.VMEM((TOK, D), BF16),
            pltpu.VMEM((D, 2 * F), BF16),
            pltpu.VMEM((F, D), BF16),
            pltpu.VMEM((2, ROWS, D), BF16),
            pltpu.VMEM((ROWS, C), F32),
            pltpu.VMEM((NCH, SLOT, C), BF16),
            pltpu.VMEM((NCH, SLOT, C), BF16),
            pltpu.VMEM((NCH, SLOT, C), BF16),
            pltpu.VMEM((NCH, NY - 1, OWN, C), BF16),
            pltpu.VMEM((ROWS, C), BF16),
            pltpu.VMEM((NZ, OWN, D), F32),
            pltpu.VMEM((NZ, NX - 1, OWN, D), BF16),
            pltpu.VMEM((NZ, NX - 1, OWN, D), BF16),
            pltpu.VMEM((OWN, D), F32),
            pltpu.VMEM((NZ - 1, OWN, D), BF16),
            pltpu.VMEM((NZ - 1, OWN, D), BF16),
            pltpu.VMEM((8, TOK), F32),
            pltpu.VMEM((2 * NY - 1, 8, TOK), F32),
            pltpu.VMEM((NX, D // 128, 128), F32),
            pltpu.VMEM((NZ, D // 128, 128), F32),
            pltpu.VMEM((TOK, 128), F32),
            pltpu.SemaphoreType.DMA((copies,)),
            pltpu.SemaphoreType.DMA((copies,)),
            pltpu.SemaphoreType.DMA((8,)),
        ],
        compiler_params=pltpu.CompilerParams(
            collective_id=0,
            has_side_effects=True,
            vmem_limit_bytes=58 * 1024 * 1024,
        ),
    )(
        hidden.reshape(slabs * rows_dev, D),
        router_weight.reshape(1, D),
        teacher,
        positions,
        cotangent,
        gate_weight,
        up_weight,
        down_weight,
    )
    hidden_grad, router_grad, gate_grad, up_grad, down_grad = store(
        (hidden_grad, router_grad, gate_grad, up_grad, down_grad)
    )
    return (
        hidden_grad.reshape(hidden.shape),
        router_grad.reshape(D),
        gate_grad,
        up_grad,
        down_grad,
    )


def solution(mesh):
    in_specs = (
        P(None, "wide", "narrow"),
        P("narrow"),
        P(None, "wide"),
        P(),
        P(None, "wide", "narrow"),
        P("narrow", "wide"),
        P("narrow", "wide"),
        P("wide", "narrow"),
    )
    out_specs = (
        P(None, "wide", "narrow"),
        P("narrow"),
        P("narrow", "wide"),
        P("narrow", "wide"),
        P("wide", "narrow"),
    )
    return jax.shard_map(
        on_device, mesh=mesh, in_specs=in_specs, out_specs=out_specs, check_vma=False
    )
```

```python
import functools

import jax
import jax.numpy as jnp
from jax import lax
from jax.experimental import pallas as pl
from jax.experimental.pallas import tpu as pltpu
from jax.sharding import PartitionSpec as P

MESH = pl.DeviceIdType.MESH
F32 = jnp.float32
BF16 = jnp.bfloat16

NX, NZ, NY = 4, 8, 4
TOK = 128
OWN = 16
ROWS = OWN * NX * NZ
SLOT = OWN * NX
CHUNKS = ((0,), (1, 2), (3, 4), (5, 6), (7,))
NCH = len(CHUNKS)
KEEPER = {0: 0, NCH - 1: 1}
EXT = 128
OFFSETS = (0, 1, -1, 2, -2, 3, -3, 4)

ORDER = (
    "GR:0", "GC:0", "A:0", "T:0", "B:0", "GR:1", "GC:1", "A:1",
    "D:0", "GR:2", "B:1", "E:0", "GC:2", "A:2", "GR:3", "B:2",
    "D:1", "F:0", "GC:3", "A:3", "G:0", "B:3", "A:4", "D:2",
    "H:0", "E:1", "B:4", "D:3", "E:2", "F:1", "D:4", "G:1",
    "E:3", "F:2", "E:4", "G:2", "F:3", "F:4", "H:1", "G:3",
    "G:4", "RX:0", "WI:0", "H:2", "WI:1", "WI:2", "WI:3", "WO:0",
    "WO:1", "H:3", "H:4", "RZ:0", "WO:2", "WO:3",
)


def encode(value, rows):
    wide = jnp.broadcast_to(value, (rows, EXT))
    high = wide.astype(BF16).astype(F32)
    lane = lax.broadcasted_iota(jnp.int32, (rows, EXT), 1)
    return jnp.where(lane < EXT // 2, high, wide - high).astype(BF16)


def decode(block):
    return block[:, 0:1].astype(F32) + block[:, EXT // 2 : EXT // 2 + 1].astype(F32)


def nt(a, b):
    return lax.dot_general(a, b, (((1,), (1,)), ((), ())), preferred_element_type=F32)


def tn(a, b):
    return lax.dot_general(a, b, (((0,), (0,)), ((), ())), preferred_element_type=F32)


def tiles(extent, step):
    return [(at, min(step, extent - at)) for at in range(0, extent, step)]


def kernel(
    D,
    F,
    hidden_hbm,
    rw_ref,
    teacher_ref,
    pos_ref,
    cot_ref,
    gw_hbm,
    uw_hbm,
    dw_hbm,
    hg_out,
    rg_ref,
    gg_out,
    ug_out,
    dg_out,
    hid,
    wgu,
    wd,
    agb,
    part,
    csend,
    crecv,
    ysend,
    yrecv,
    gact,
    rgf,
    xsend,
    xrecv,
    zown,
    zsend,
    zrecv,
    lsend,
    lrecv,
    rparts_x,
    rparts_z,
    tgrad,
    send_sem,
    recv_sem,
    local_sem,
):
    C = 3 * F + EXT
    H = C // 2
    wide, narrow = lax.axis_index("wide"), lax.axis_index("narrow")
    x, z = lax.div(wide, NZ), lax.rem(wide, NZ)
    y, core = lax.div(narrow, 2), lax.rem(narrow, 2)

    def at_x(d):
        return (lax.rem(x + d + NX, NX) * NZ + z, narrow)

    def at_z(d):
        return (x * NZ + lax.rem(z + d + NZ, NZ), narrow)

    def at_y(d):
        return (wide, lax.rem(y + d + NY, NY) * 2 + core)

    def at_n(d):
        return (wide, lax.rem(narrow + d, 2 * NY))

    sibling = (wide, y * 2 + (1 - core))

    count = [0]
    started = []

    def make(src, dst, device):
        i = count[0]
        count[0] += 1
        return pltpu.make_async_remote_copy(
            src_ref=src,
            dst_ref=dst,
            send_sem=send_sem.at[i],
            recv_sem=recv_sem.at[i],
            device_id=device,
            device_id_type=MESH,
        )

    def send(src, dst, device):
        copy = make(src, dst, device)
        copy.start()
        started.append(copy)
        return copy

    def on(core_of_chip, part):
        if core_of_chip is None:
            part()
        else:
            pl.when(core == core_of_chip)(part)

    lcount = [0]

    def local(src, dst):
        copy = pltpu.make_async_copy(src, dst, local_sem.at[lcount[0]])
        lcount[0] += 1
        copy.start()
        return copy

    load_hid = local(hidden_hbm, hid)
    load_w = [
        local(gw_hbm, wgu.at[:, pl.ds(0, F)]),
        local(uw_hbm, wgu.at[:, pl.ds(F, F)]),
        local(dw_hbm, wd),
    ]

    barrier = pltpu.get_barrier_semaphore()
    peers = (
        [at_x(d) for d in range(1, NX)]
        + [at_z(d) for d in range(1, NZ)]
        + [at_n(d) for d in range(1, 2 * NY)]
    )
    for peer in peers:
        pl.semaphore_signal(barrier, inc=1, device_id=peer, device_id_type=MESH)

    sub = lax.broadcasted_iota(jnp.int32, (OWN, TOK), 0)
    lane = lax.broadcasted_iota(jnp.int32, (OWN, TOK), 1)
    sub_t = lax.broadcasted_iota(jnp.int32, (TOK, OWN), 0)
    lane_t = lax.broadcasted_iota(jnp.int32, (TOK, OWN), 1)
    pick = jnp.zeros((OWN, TOK), F32)
    place = jnp.zeros((TOK, OWN), F32)
    half_own, half_tok = OWN // 2, TOK // 2
    for r in range(OWN):
        s, j = r // half_own, r % half_own
        token = pos_ref[s, wide * half_own + j] - wide * half_tok + s * half_tok
        pick = jnp.where((sub == r) & (lane == token), 1.0, pick)
        place = jnp.where((lane_t == r) & (sub_t == token), 1.0, place)
    load_hid.wait()
    own_rows = jnp.dot(pick.astype(BF16), hid[...], preferred_element_type=F32)
    agb[0, pl.ds(0, OWN), :] = own_rows.astype(BF16)
    agb[1, pl.ds(0, OWN), :] = jnp.concatenate(
        [cot_ref[0].astype(F32), cot_ref[1].astype(F32)], axis=0
    ).astype(BF16)
    pl.semaphore_wait(barrier, len(peers))

    def gather_x(which):
        own = agb.at[which, pl.ds(0, OWN)]
        return [
            send(own, agb.at[which, pl.ds((NX - d) * OWN, OWN)], at_x(d)) for d in (2, 1, 3)
        ]

    gx = {0: gather_x(0)}

    eye = lax.broadcasted_iota(jnp.int32, (TOK, TOK), 0) == lax.broadcasted_iota(
        jnp.int32, (TOK, TOK), 1
    )
    logit_col = jnp.sum(hid[...].astype(F32) * rw_ref[...], axis=1, keepdims=True)
    logit_row = jnp.sum(jnp.where(eye, logit_col, 0.0), axis=0, keepdims=True)
    lsend[...] = jnp.broadcast_to(logit_row, (8, TOK))
    gx[1] = gather_x(1)
    lg = [send(lsend, lrecv.at[d - 1], at_n(d)) for d in range(1, 2 * NY)]

    gz = {}

    def ring(which, src, dst, d, at=0, n=SLOT):
        return send(
            agb.at[which, pl.ds(src * SLOT + at, n)],
            agb.at[which, pl.ds(dst * SLOT + at, n)],
            at_z(d),
        )

    def gather(which, step):
        for copy in gx[which] if step == 0 else gz[which, step]:
            copy.wait_recv()
        if step == 0:
            gz[which, 1] = [ring(which, 0, 1, -1), ring(which, 0, 2, 1)]
        elif step == 1:
            gz[which, 2] = [ring(which, 1, 3, -1), ring(which, 2, 4, 1)]
        elif step == 2:
            gz[which, 3] = [ring(which, 3, 5, -1), ring(which, 4, 6, 1)]
        elif step == 3:
            half = SLOT // 2
            gz[which, 4] = [
                ring(which, 5, 7, -1, 0, half),
                ring(which, 6, 7, 1, half, half),
            ]

    core_out, y_out, g_first, g_second, core_back, x_out, z_out = ({} for _ in range(7))

    def block(j, base=0):
        return pl.ds(pl.multiple_of(base + lax.rem(y + j + NY, NY) * OWN, OWN), OWN)

    def chunk(i):
        base, rows = CHUNKS[i][0] * SLOT, len(CHUNKS[i]) * SLOT
        keeper = KEEPER.get(i)
        share = base if keeper is not None else base + core * SLOT
        return keeper, base, rows, share

    def stage1(i):
        keeper, base, n, _ = chunk(i)
        rows = pl.ds(base, n)
        if i == 0:
            for copy in load_w:
                copy.wait()
        if i == NCH - 1:
            for which in (0, 1):
                for copy in gz[which, 4]:
                    copy.wait_recv()
        for at, m in tiles(2 * F, 256):
            cols = pl.ds(at, m)
            part[rows, cols] = jnp.dot(
                agb[0, rows, :], wgu[:, cols], preferred_element_type=F32
            )
        for at, m in tiles(F, 256):
            part[rows, pl.ds(2 * F + at, m)] = nt(agb[1, rows, :], wd[pl.ds(at, m), :])
        logit = jnp.sum(agb[0, rows, :].astype(F32) * rw_ref[...], axis=1, keepdims=True)
        part[rows, pl.ds(3 * F, EXT)] = jnp.broadcast_to(logit, (n, EXT))
        if keeper is None:
            other = pl.ds(pl.multiple_of(base + (1 - core) * SLOT, SLOT), SLOT)
        else:
            other = rows
        copy = make(csend.at[i], crecv.at[i], sibling)
        core_out[i] = copy

        def to_other():
            csend[i, :, pl.ds(0, 3 * F)] = part[other, pl.ds(0, 3 * F)].astype(BF16)
            csend[i, :, pl.ds(3 * F, EXT)] = encode(
                part[other, pl.ds(3 * F, EXT)][:, 0:1], SLOT
            )
            copy.start()

        on(None if keeper is None else 1 - keeper, to_other)

    def stage2(i):
        keeper, _, _, share = chunk(i)
        mine = pl.ds(share if keeper is not None else pl.multiple_of(share, SLOT), SLOT)
        copies = [
            make(ysend.at[i, block(d)], yrecv.at[i, d - 1], at_y(d)) for d in (2, 1, 3)
        ]
        y_out[i] = copies

        def add():
            core_out[i].wait_recv()
            total = part[mine, pl.ds(0, 3 * F)] + crecv[i, :, pl.ds(0, 3 * F)].astype(F32)
            part[mine, pl.ds(0, 3 * F)] = total
            ysend[i, :, pl.ds(0, 3 * F)] = total.astype(BF16)
            logit = part[mine, pl.ds(3 * F, EXT)][:, 0:1] + decode(
                crecv[i, :, pl.ds(3 * F, EXT)]
            )
            part[mine, pl.ds(3 * F, EXT)] = jnp.broadcast_to(logit, (SLOT, EXT))
            ysend[i, :, pl.ds(3 * F, EXT)] = encode(logit, SLOT)
            for copy in copies:
                copy.start()

        on(keeper, add)

    def stage4(i):
        keeper, _, _, share = chunk(i)
        own = block(0, share)
        ext = pl.ds(3 * F, EXT)
        copies = [make(gact.at[own], gact.at[own], at_y(d)) for d in (1, -1)]
        g_first[i] = copies

        def gate_block():
            for copy in y_out[i]:
                copy.wait_recv()

            def total(at):
                cols = pl.ds(at, F)
                value = part[own, cols]
                for d in range(NY - 1):
                    value = value + yrecv[i, d, :, cols].astype(F32)
                return value

            logit = part[own, ext][:, 0:1]
            for d in range(NY - 1):
                logit = logit + decode(yrecv[i, d, :, ext])
            scale = jax.nn.sigmoid(logit)
            gate, up, raw = total(0), total(F), total(2 * F)
            sig = jax.nn.sigmoid(gate)
            silu = gate * sig
            act = silu * up
            act_grad = scale * raw
            gate_pre = act_grad * up * sig * (1.0 + gate * (1.0 - sig))
            gact[own, pl.ds(0, F)] = gate_pre.astype(BF16)
            gact[own, pl.ds(F, F)] = (act_grad * silu).astype(BF16)
            gact[own, pl.ds(2 * F, F)] = (scale * act).astype(BF16)
            dots = jnp.sum(act * raw, axis=1, keepdims=True)
            gact[own, ext] = encode(scale * (1.0 - scale) * dots, OWN)
            for copy in copies:
                copy.start()

        on(keeper, gate_block)

    def stage5(i):
        keeper, _, _, share = chunk(i)
        left = gact.at[block(-1, share), pl.ds(0, H)]
        right = gact.at[block(1, share), pl.ds(H, H)]
        copies = [make(left, left, at_y(1)), make(right, right, at_y(-1))]
        g_second[i] = copies

        def hand_on():
            for first, second in zip(g_first[i], copies):
                first.wait_recv()
                second.start()

        on(keeper, hand_on)

    def stage6(i):
        keeper, _, _, share = chunk(i)
        start = share if keeper is not None else pl.multiple_of(share, SLOT)
        half = gact.at[pl.ds(start, SLOT)]
        copy = make(half, half, sibling)
        core_back[i] = copy

        def give():
            for second in g_second[i]:
                second.wait_recv()
            copy.start()

        on(keeper, give)

    def stage7(i):
        keeper, base, n, _ = chunk(i)
        on(None if keeper is None else 1 - keeper, core_back[i].wait_recv)
        rows = pl.ds(base, n)
        routed = decode(gact[rows, pl.ds(3 * F, EXT)])
        for at, m in tiles(D, 256):
            cols = pl.ds(at, m)
            out = nt(gact[rows, pl.ds(0, 2 * F)], wgu[cols, :]) + routed * rw_ref[:, cols]
            for s, k in enumerate(CHUNKS[i]):
                for j in range(NX):
                    piece = out[s * SLOT + j * OWN : s * SLOT + (j + 1) * OWN]
                    if j == 0:
                        rgf[k, :, cols] = piece
                    else:
                        xsend[k, j - 1, :, cols] = piece.astype(BF16)
        slots = pl.ds(CHUNKS[i][0], len(CHUNKS[i]))
        x_out[i] = [
            send(xsend.at[slots, j - 1], xrecv.at[slots, j - 1], at_x(j)) for j in (2, 1, 3)
        ]

    def stage8(i):
        for copy in x_out[i]:
            copy.wait_recv()
        for k in CHUNKS[i]:
            total = rgf[k]
            for j in range(NX - 1):
                total = total + xrecv[k, j].astype(F32)
            if k == 0:
                zown[...] = total
            else:
                zsend[k - 1] = total.astype(BF16)
                z_out[k] = send(zsend.at[k - 1], zrecv.at[k - 1], at_z(OFFSETS[k]))

    held = {}

    def own_tokens():
        for copy in lg:
            copy.wait_recv()
        logits = lsend[0:1, :]
        for d in range(2 * NY - 1):
            logits = logits + lrecv[d, 0:1, :]
        logit_col = jnp.sum(jnp.where(eye, logits, 0.0), axis=1, keepdims=True)
        eye_half = lax.broadcasted_iota(jnp.int32, (half_tok, half_tok), 0) == (
            lax.broadcasted_iota(jnp.int32, (half_tok, half_tok), 1)
        )
        teacher = jnp.concatenate(
            [
                jnp.sum(jnp.where(eye_half, teacher_ref[s : s + 1, :], 0.0), axis=1, keepdims=True)
                for s in range(2)
            ],
            axis=0,
        )
        grad = jax.nn.sigmoid(logit_col) - teacher
        router = jnp.sum(grad * hid[...].astype(F32), axis=0, keepdims=True)
        for a in range(D // 128):
            rparts_x[x, a : a + 1, :] = router[:, a * 128 : (a + 1) * 128]
        tgrad[...] = jnp.broadcast_to(grad, (TOK, 128))

    def router_x():
        routed = tn(gact[:, pl.ds(3 * F, EXT)], agb[0])
        routed = routed[0:1] + routed[EXT // 2 : EXT // 2 + 1]
        for a in range(D // 128):
            rparts_x[x, a : a + 1, :] += routed[:, a * 128 : (a + 1) * 128]
        held["rx"] = [send(rparts_x.at[x], rparts_x.at[x], at_x(d)) for d in range(1, NX)]

    def router_z():
        for copy in held["rx"]:
            copy.wait_recv()
        rparts_z[z] = rparts_x[0] + rparts_x[1] + rparts_x[2] + rparts_x[3]
        held["rz"] = [send(rparts_z.at[z], rparts_z.at[z], at_z(d)) for d in range(1, NZ)]

    def grads_in(t):
        cols = pl.ds(t * 256, 256)
        out = tn(agb[0, :, cols], gact[:, pl.ds(0, 2 * F)])
        gg_out[cols, :] = out[:, :F].astype(BF16)
        ug_out[cols, :] = out[:, F:].astype(BF16)

    def grads_out(t):
        at, n = tiles(F, 256)[t]
        dg_out[pl.ds(at, n), :] = tn(gact[:, pl.ds(2 * F + at, n)], agb[1]).astype(BF16)

    tasks = {
        "GR": lambda step: gather(0, step),
        "GC": lambda step: gather(1, step),
        "A": stage1,
        "B": stage2,
        "D": stage4,
        "E": stage5,
        "F": stage6,
        "G": stage7,
        "H": stage8,
        "T": lambda _: own_tokens(),
        "RX": lambda _: router_x(),
        "RZ": lambda _: router_z(),
        "WI": grads_in,
        "WO": grads_out,
    }
    for task in ORDER:
        name, step = task.split(":")
        tasks[name](int(step))

    late = list(z_out.values()) + held["rz"]
    late_ids = [id(copy) for copy in late]
    for copy in started:
        if id(copy) not in late_ids:
            copy.wait_send()
    for i in range(NCH):
        keeper = KEEPER.get(i)

        def sent(keeper=keeper, i=i):
            for copy in y_out[i] + g_first[i] + g_second[i] + [core_back[i]]:
                copy.wait_send()

        on(keeper, sent)
        on(None if keeper is None else 1 - keeper, core_out[i].wait_send)

    for k in range(1, NZ):
        z_out[k].wait_recv()
    total = zown[...]
    for k in range(NZ - 1):
        total = total + zrecv[k].astype(F32)
    high = total.astype(BF16)
    low = (total - high.astype(F32)).astype(BF16)
    place16 = place.astype(BF16)
    hg_out[...] = (
        tgrad[:, 0:1] * rw_ref[...]
        + jnp.dot(place16, high, preferred_element_type=F32)
        + jnp.dot(place16, low, preferred_element_type=F32)
    ).astype(BF16)

    for copy in held["rz"]:
        copy.wait_recv()
    final = rparts_z[0]
    for k in range(1, NZ):
        final = final + rparts_z[k]
    for a in range(D // 128):
        rg_ref[:, a * 128 : (a + 1) * 128] = final[a : a + 1, :]

    for copy in late:
        copy.wait_send()


def store_kernel(*refs):
    n = len(refs) // 2
    sems = refs[-1]
    copies = [pltpu.make_async_copy(refs[i], refs[n + i], sems.at[i]) for i in range(n)]
    for copy in copies:
        copy.start()
    for copy in copies:
        copy.wait()


def store(arrays):
    arrays = [pltpu.with_memory_space_constraint(a, pltpu.VMEM) for a in arrays]
    return pl.pallas_call(
        store_kernel,
        out_shape=tuple(jax.ShapeDtypeStruct(a.shape, a.dtype) for a in arrays),
        in_specs=[pl.BlockSpec(memory_space=pltpu.VMEM)] * len(arrays),
        out_specs=(pl.BlockSpec(memory_space=pl.ANY),) * len(arrays),
        scratch_shapes=[pltpu.SemaphoreType.DMA((len(arrays),))],
        compiler_params=pltpu.CompilerParams(vmem_limit_bytes=8 * 1024 * 1024),
    )(*arrays)


def on_device(
    hidden, router_weight, teacher, positions, cotangent, gate_weight, up_weight, down_weight
):
    slabs, rows_dev, D = hidden.shape
    F = gate_weight.shape[1]
    C = 3 * F + EXT
    vmem = pl.BlockSpec(memory_space=pltpu.VMEM)
    smem = pl.BlockSpec(memory_space=pltpu.SMEM)
    hbm = pl.BlockSpec(memory_space=pl.ANY)
    copies = 6 + 16 + 7 + NCH * 12 + 7 + 3 + 7
    hidden_grad, router_grad, gate_grad, up_grad, down_grad = pl.pallas_call(
        functools.partial(kernel, D, F),
        out_shape=(
            pltpu.VMEM((TOK, D), BF16),
            pltpu.VMEM((1, D), F32),
            pltpu.VMEM((D, F), BF16),
            pltpu.VMEM((D, F), BF16),
            pltpu.VMEM((F, D), BF16),
        ),
        in_specs=[hbm, vmem, vmem, smem, vmem, hbm, hbm, hbm],
        out_specs=(vmem,)*5,
        scratch_shapes=[
            pltpu.VMEM((TOK, D), BF16),
            pltpu.VMEM((D, 2 * F), BF16),
            pltpu.VMEM((F, D), BF16),
            pltpu.VMEM((2, ROWS, D), BF16),
            pltpu.VMEM((ROWS, C), F32),
            pltpu.VMEM((NCH, SLOT, C), BF16),
            pltpu.VMEM((NCH, SLOT, C), BF16),
            pltpu.VMEM((NCH, SLOT, C), BF16),
            pltpu.VMEM((NCH, NY - 1, OWN, C), BF16),
            pltpu.VMEM((ROWS, C), BF16),
            pltpu.VMEM((NZ, OWN, D), F32),
            pltpu.VMEM((NZ, NX - 1, OWN, D), BF16),
            pltpu.VMEM((NZ, NX - 1, OWN, D), BF16),
            pltpu.VMEM((OWN, D), F32),
            pltpu.VMEM((NZ - 1, OWN, D), BF16),
            pltpu.VMEM((NZ - 1, OWN, D), BF16),
            pltpu.VMEM((8, TOK), F32),
            pltpu.VMEM((2 * NY - 1, 8, TOK), F32),
            pltpu.VMEM((NX, D // 128, 128), F32),
            pltpu.VMEM((NZ, D // 128, 128), F32),
            pltpu.VMEM((TOK, 128), F32),
            pltpu.SemaphoreType.DMA((copies,)),
            pltpu.SemaphoreType.DMA((copies,)),
            pltpu.SemaphoreType.DMA((8,)),
        ],
        compiler_params=pltpu.CompilerParams(
            collective_id=0,
            has_side_effects=True,
            vmem_limit_bytes=58 * 1024 * 1024,
        ),
    )(
        hidden.reshape(slabs * rows_dev, D),
        router_weight.reshape(1, D),
        teacher,
        positions,
        cotangent,
        gate_weight,
        up_weight,
        down_weight,
    )
    hidden_grad, router_grad, gate_grad, up_grad, down_grad = store(
        (hidden_grad, router_grad, gate_grad, up_grad, down_grad)
    )
    return (
        hidden_grad.reshape(hidden.shape),
        router_grad.reshape(D),
        gate_grad,
        up_grad,
        down_grad,
    )


def solution(mesh):
    in_specs = (
        P(None, "wide", "narrow"),
        P("narrow"),
        P(None, "wide"),
        P(),
        P(None, "wide", "narrow"),
        P("narrow", "wide"),
        P("narrow", "wide"),
        P("wide", "narrow"),
    )
    out_specs = (
        P(None, "wide", "narrow"),
        P("narrow"),
        P("narrow", "wide"),
        P("narrow", "wide"),
        P("wide", "narrow"),
    )
    return jax.shard_map(
        on_device, mesh=mesh, in_specs=in_specs, out_specs=out_specs, check_vma=False
    )
```
